512 devices in a mesh: sec: 8 (over x, core), xy: 64 (over y, z).
Axes of the slice: x: 4, y: 8, z: 8, core: 2. Of those that a mesh axis runs over, the one named last changes fastest.
Arguments:
- patches: bfloat16 [16, 64, 8, 160, 160], P('sec', 'xy'), may hold values from -100 to 100
- margins: bfloat16 [16, 64, 6, 160, 160], P('sec', 'xy'), may hold values from -100 to 100
- offsets: int32 [16, 64, 8, 2], P('sec', 'xy'), may hold values from -40 to 40
- counts: int32 [16, 64], P('sec', 'xy'), may hold values from 1 to 8
Outputs:
- flow: float32 [16, 64, 2, 8], P('sec', 'xy')
- seams: float32 [16, 64, 2, 6], P('sec', 'xy')
The draws below stay inside these ranges and needn't reach their ends.
All inputs are finite; a program needn't handle non-finite values.
Results may differ from the reference program's by a relative error of at most 0.022.
The reference program's roundings to bfloat16 on the way (of `normal_patch`) count: a program that leaves them out, or rounds other values in their place, can miss the bound.
Values may be sent and summed in bfloat16 or wider, within the bound.
A program may use at most 64 MiB of HBM per device.

```python
import jax
import jax.numpy as jnp
from jax import lax

SIDE = 160
PATCH_ROWS = 2
PATCH_COLS = 4
GRID_COLS = 4
OFFSET_MAX = 40
NSEC = 16
NXY = 64


def drawn(key):
    keys = jax.random.split(key, 10)
    slot_count = PATCH_ROWS * PATCH_COLS
    shape = (NSEC, NXY, slot_count, SIDE, SIDE)
    noise = jnp.clip(jax.random.normal(keys[0], shape, jnp.float32), -6.0, 6.0)
    raw = noise
    level = jax.random.uniform(keys[4], (NSEC, NXY, slot_count, 1, 1), jnp.float32, -2.0, 2.0)
    gain = jax.random.uniform(keys[5], (NSEC, NXY, slot_count, 1, 1), jnp.float32, 0.5, 2.0)
    images = level + gain * raw
    edge_shape = (NSEC, NXY, PATCH_ROWS + PATCH_COLS, SIDE, SIDE)
    edge_noise = jnp.clip(jax.random.normal(keys[6], edge_shape, jnp.float32), -6.0, 6.0)
    edge_level = jax.random.uniform(keys[8], edge_shape[:3] + (1, 1), jnp.float32, -2.0, 2.0)
    edge_gain = jax.random.uniform(keys[9], edge_shape[:3] + (1, 1), jnp.float32, 0.5, 2.0)
    margins = edge_level + edge_gain * edge_noise
    return (images, margins)


def draw_patches(key, part):
    images = drawn(key)[0]
    return images.astype(jnp.bfloat16)


def draw_margins(key, part):
    edges = drawn(key)[1]
    return edges.astype(jnp.bfloat16)


def with_ends(result, key, smallest, top_value):
    longest = result.shape.index(max(result.shape))
    spots = []
    for shift in (0, 1):
        where = [jax.random.randint(jax.random.fold_in(key, axis), (), 0, length) for axis, length in enumerate(result.shape)]
        where[longest] = (where[longest] + shift) % result.shape[longest]
        spots.append(tuple(where))
    return result.at[spots[0]].set(smallest).at[spots[1]].set(top_value)


def setup_inputs(seed: int = 0) -> dict:
    key_of = jax.random.split(jax.random.key(seed), 5)
    patches = draw_patches(jax.random.fold_in(key_of[4], 71), 0)
    margins = draw_margins(jax.random.fold_in(key_of[4], 71), 0)
    offsets = with_ends(jax.random.randint(key_of[2], (NSEC, NXY, PATCH_ROWS * PATCH_COLS, 2), 0 - OFFSET_MAX, OFFSET_MAX + 1), jax.random.fold_in(key_of[2], 1), 0 - OFFSET_MAX, OFFSET_MAX).astype(jnp.int32)
    counts = with_ends(jax.random.randint(key_of[3], (NSEC, NXY), 1, PATCH_ROWS * PATCH_COLS + 1), jax.random.fold_in(key_of[3], 1), 1, PATCH_ROWS * PATCH_COLS).astype(jnp.int32)
    return {"patches": patches, "margins": margins, "offsets": offsets, "counts": counts}


pixel_unit = 16.0

def dft_tables(length):
    freq = jnp.arange(length, dtype=jnp.int32)
    phase = freq[:, None] * freq[None, :] % length
    angle = phase.astype(jnp.float32) * (2.0 * jnp.pi / length)
    return (jnp.cos(angle).astype(jnp.bfloat16), jnp.sin(angle).astype(jnp.bfloat16))

def right_mul(images, table):
    return jnp.einsum('...ij,jk->...ik', images.astype(jnp.float32), table.astype(jnp.float32), precision=lax.Precision.HIGHEST)

def left_mul(table, images):
    return jnp.einsum('ij,...jk->...ik', table.astype(jnp.float32), images.astype(jnp.float32), precision=lax.Precision.HIGHEST)

def spectrum(images, cosine, sine_table):
    values = images.astype(jnp.float32)
    centred = values - lax.optimization_barrier(jnp.mean(values, axis=(-2, -1), keepdims=True))
    spread = jnp.sqrt(lax.optimization_barrier(jnp.mean(centred * centred, axis=(-2, -1), keepdims=True)) + 1e-05)
    normal_patch = (centred / spread).astype(jnp.bfloat16)
    rows_cos = right_mul(normal_patch, cosine).astype(jnp.bfloat16)
    rows_sin = right_mul(normal_patch, sine_table).astype(jnp.bfloat16)
    spec_re = (left_mul(cosine, rows_cos) - left_mul(sine_table, rows_sin)).astype(jnp.bfloat16)
    spec_im = (-(left_mul(sine_table, rows_cos) + left_mul(cosine, rows_sin))).astype(jnp.bfloat16)
    return (spec_re, spec_im)

def displacement(source_pair, target_pair, centre, cosine, sine_table):
    a_re = source_pair[0].astype(jnp.float32)
    a_im = source_pair[1].astype(jnp.float32)
    b_re = target_pair[0].astype(jnp.float32)
    b_im = target_pair[1].astype(jnp.float32)
    cross_re = (a_re * b_re + a_im * b_im).astype(jnp.bfloat16)
    cross_im = (a_im * b_re - a_re * b_im).astype(jnp.bfloat16)
    back_u = (right_mul(cross_re, cosine) - right_mul(cross_im, sine_table)).astype(jnp.bfloat16)
    back_v = (right_mul(cross_re, sine_table) + right_mul(cross_im, cosine)).astype(jnp.bfloat16)
    side = cross_re.shape[-1]
    scores = (left_mul(cosine, back_u) - left_mul(sine_table, back_v)) * (2.0 / float(side) ** 3)
    largest = lax.optimization_barrier(jnp.max(scores, axis=(-2, -1), keepdims=True))
    weights = jnp.exp(scores - largest)
    weights = weights / lax.optimization_barrier(jnp.sum(weights, axis=(-2, -1), keepdims=True))
    half_side = side // 2
    positions = jnp.arange(side, dtype=jnp.int32)
    centre_rows = centre[..., 0:1].astype(jnp.int32)
    centre_cols = centre[..., 1:2].astype(jnp.int32)
    label_rows = centre_rows + jnp.remainder(positions - centre_rows + half_side, side) - half_side
    label_cols = centre_cols + jnp.remainder(positions - centre_cols + half_side, side) - half_side
    flow_rows = lax.optimization_barrier(jnp.sum(lax.optimization_barrier(jnp.sum(weights, axis=-1)) * label_rows.astype(jnp.float32), axis=-1))
    flow_cols = lax.optimization_barrier(jnp.sum(lax.optimization_barrier(jnp.sum(weights, axis=-2)) * label_cols.astype(jnp.float32), axis=-1))
    return jnp.stack([flow_rows, flow_cols], axis=-1) / pixel_unit

def reference(patches, margins, offsets, counts):
    cosine, sine_table = dft_tables(SIDE)
    slot_count = PATCH_ROWS * PATCH_COLS
    slot_ids = jnp.arange(slot_count, dtype=jnp.int32)
    tile_ids = jnp.arange(NXY, dtype=jnp.int32)
    tile_column = tile_ids % GRID_COLS
    edge_slots = jnp.concatenate([jnp.arange(PATCH_ROWS, dtype=jnp.int32) * PATCH_COLS + PATCH_COLS - 1, (PATCH_ROWS - 1) * PATCH_COLS + jnp.arange(PATCH_COLS, dtype=jnp.int32)])
    seam_usable = jnp.concatenate([jnp.broadcast_to((tile_column < GRID_COLS - 1)[:, None], (NXY, PATCH_ROWS)), jnp.broadcast_to((tile_ids < NXY - GRID_COLS)[:, None], (NXY, PATCH_COLS))], axis=1).astype(jnp.float32)

    def one_section(section):
        here = spectrum(patches[section], cosine, sine_table)
        following = spectrum(patches[jnp.minimum(section + 1, NSEC - 1)], cosine, sine_table)
        cross = displacement(here, following, offsets[section], cosine, sine_table)
        usable = ((slot_ids[None, :] < counts[section][:, None]) & (section < NSEC - 1)).astype(jnp.float32)
        cross = cross * usable[..., None]
        margin_block = margins[section]
        right_in = jnp.roll(margin_block[:, :PATCH_ROWS], -1, axis=0)
        lower_in = jnp.roll(margin_block[:, PATCH_ROWS:], -GRID_COLS, axis=0)
        received = spectrum(jnp.concatenate([right_in, lower_in], axis=1), cosine, sine_table)
        own_edges = (here[0][:, edge_slots], here[1][:, edge_slots])
        centres = jnp.zeros((NXY, PATCH_ROWS + PATCH_COLS, 2), jnp.int32)
        seam = displacement(own_edges, received, centres, cosine, sine_table) * seam_usable[..., None]
        return (cross, usable, seam)
    cross, usable, seam = lax.map(one_section, jnp.arange(NSEC, dtype=jnp.int32))
    grid_rows = NXY // GRID_COLS
    mesh_flow = cross.reshape(NSEC, grid_rows, GRID_COLS, PATCH_ROWS, PATCH_COLS, 2)
    mesh_flow = mesh_flow.transpose(0, 5, 1, 3, 2, 4).reshape(NSEC, 2, grid_rows * PATCH_ROWS, GRID_COLS * PATCH_COLS)
    mesh_mark = usable.reshape(NSEC, grid_rows, GRID_COLS, PATCH_ROWS, PATCH_COLS)
    mesh_mark = mesh_mark.transpose(0, 1, 3, 2, 4).reshape(NSEC, grid_rows * PATCH_ROWS, GRID_COLS * PATCH_COLS)
    padded_flow = jnp.pad(mesh_flow, ((0, 0), (0, 0), (1, 1), (1, 1)))
    padded_mark = jnp.pad(mesh_mark, ((0, 0), (1, 1), (1, 1)))
    beside_flow = padded_flow[..., 2:, 1:-1] + padded_flow[..., :-2, 1:-1] + padded_flow[..., 1:-1, 2:] + padded_flow[..., 1:-1, :-2]
    beside_mark = padded_mark[..., 2:, 1:-1] + padded_mark[..., :-2, 1:-1] + padded_mark[..., 1:-1, 2:] + padded_mark[..., 1:-1, :-2]
    smooth = mesh_mark[:, None] * (2.0 * mesh_flow + beside_flow) / (2.0 + beside_mark[:, None])
    smooth = smooth.reshape(NSEC, 2, grid_rows, PATCH_ROWS, GRID_COLS, PATCH_COLS).transpose(0, 2, 4, 1, 3, 5)
    flow = smooth.reshape(NSEC, NXY, 2, slot_count)
    seams = seam.transpose(0, 1, 3, 2)
    return (flow, seams)
```

```python
import functools

import jax
import jax.numpy as jnp
import ml_dtypes
import numpy as np
from jax import lax
from jax.experimental import pallas as pl
from jax.experimental.pallas import tpu as pltpu
from jax.sharding import PartitionSpec as P

SIDE = 160
HALF = SIDE // 2
PATCH_ROWS = 2
PATCH_COLS = 4
GRID_COLS = 4
SLOTS = PATCH_ROWS * PATCH_COLS
EDGES = PATCH_ROWS + PATCH_COLS
LANES = 128
TAIL = SIDE - LANES
GROUP = 4
BAND = 96
PIXEL_UNIT = 16.0
LOG2E = 1.4426950408889634
SCORE_SCALE = 2.0 / float(SIDE) ** 3
EXP2_SCALE = SCORE_SCALE * LOG2E

T_ROW = 0
WRE_ROW = T_ROW + GROUP * 256
WIM_ROW = WRE_ROW + 256
CS_ROW = WIM_ROW + 256
BACK_ROW = CS_ROW + 2 * BAND
TABLE_ROWS = BACK_ROW + SIDE

NEXT = 16
LEFT = 24
BELOW = 28
IMAGES = 36
PAIRS = 28
PAIR_ROWS = 32

MESH = pl.DeviceIdType.MESH


def tables():
    freq = np.arange(SIDE)
    phase = (freq[:, None] * freq[None, :]) % SIDE
    angle = phase.astype(np.float32) * np.float32(2.0 * np.pi / SIDE)
    cosine = np.cos(angle).astype(ml_dtypes.bfloat16).astype(np.float32)
    sine = np.sin(angle).astype(ml_dtypes.bfloat16).astype(np.float32)
    n = HALF + 1
    out = np.zeros((TABLE_ROWS, 256), np.float32)
    right = np.zeros((SIDE, 256), np.float32)
    right[:, :n] = cosine[:, :n]
    right[:, 128 : 128 + n] = sine[:, :n]
    for p in range(GROUP):
        base = T_ROW + 256 * p
        out[base : base + LANES] = right[:LANES]
        low = base + LANES + TAIL * p
        out[low : low + TAIL] = right[LANES:]
    inner = np.ones((n, 1), np.float32)
    inner[0] = inner[HALF] = 0.0
    cos_half, sin_half = cosine[:n, :n], sine[:n, :n]
    out[WRE_ROW : WRE_ROW + n, :n] = cos_half
    out[WRE_ROW + 128 : WRE_ROW + 128 + n, :n] = cos_half * inner
    out[WRE_ROW : WRE_ROW + n, 128 : 128 + n] = sin_half
    out[WRE_ROW + 128 : WRE_ROW + 128 + n, 128 : 128 + n] = -sin_half * inner
    out[WIM_ROW : WIM_ROW + n, :n] = sin_half
    out[WIM_ROW + 128 : WIM_ROW + 128 + n, :n] = sin_half * inner
    out[WIM_ROW : WIM_ROW + n, 128 : 128 + n] = cos_half
    out[WIM_ROW + 128 : WIM_ROW + 128 + n, 128 : 128 + n] = -cos_half * inner
    out[CS_ROW : CS_ROW + n, :SIDE] = cosine[:n]
    out[CS_ROW + BAND : CS_ROW + BAND + n, :SIDE] = sine[:n]
    twice = 1.0 + inner[:, 0]
    out[BACK_ROW : BACK_ROW + SIDE, :n] = cosine[:, :n] * twice
    out[BACK_ROW : BACK_ROW + SIDE, BAND : BAND + n] = -sine[:, :n] * twice
    return out.astype(ml_dtypes.bfloat16)


def iota(shape, axis):
    return lax.broadcasted_iota(jnp.int32, shape, axis)


def dot(a, b):
    return jnp.dot(a, b, preferred_element_type=jnp.float32)


def wrapped(index, centre):
    return jnp.where(index >= centre + HALF, index - SIDE, index).astype(jnp.float32)


def kernel(
    sections,
    patches,
    margins,
    table_in,
    offsets,
    counts,
    flow_out,
    seams_out,
    table,
    main,
    rem,
    raw,
    spec,
    peak,
    total,
    moment,
    centre,
    mesh_own,
    mesh_in,
    local_sem,
    send_sem,
    recv_sem,
    mesh_send,
    mesh_recv,
):
    sec = lax.axis_index("sec")
    tile = lax.axis_index("xy")
    sec_total = lax.axis_size("sec")
    tile_total = lax.axis_size("xy")
    column = lax.rem(tile, GRID_COLS)
    has_before = sec > 0
    has_after = sec < sec_total - 1
    has_left = column > 0
    has_right = column < GRID_COLS - 1
    has_above = tile >= GRID_COLS
    has_below = tile < tile_total - GRID_COLS

    local_copies = []

    def fetch(src, dst):
        copy = pltpu.make_async_copy(src, dst, local_sem.at[len(local_copies)])
        copy.start()
        local_copies.append(copy)
        return copy

    margin_raw = [
        fetch(margins.at[k, 0, :, :, pl.ds(LANES, TAIL)], raw.at[pl.ds(16 + EDGES * k, EDGES)])
        for k in range(sections)
    ]
    table_copy = fetch(table_in, table)
    patch_raw = [
        fetch(patches.at[k, 0, :, :, pl.ds(LANES, TAIL)], raw.at[pl.ds(SLOTS * k, SLOTS)])
        for k in range(sections)
    ]
    patch_main = [
        fetch(patches.at[k, 0, :, :, pl.ds(0, LANES)], main.at[pl.ds(SLOTS * k, SLOTS)])
        for k in range(sections)
    ]

    barrier = pltpu.get_barrier_semaphore()
    peers = (
        (has_before, (sec - 1, tile)),
        (has_after, (sec + 1, tile)),
        (has_left, (sec, tile - 1)),
        (has_right, (sec, tile + 1)),
        (has_above, (sec, tile - GRID_COLS)),
        (has_below, (sec, tile + GRID_COLS)),
    )
    for there, device in peers:

        @pl.when(there)
        def _(device=device):
            pl.semaphore_signal(barrier, inc=1, device_id=device, device_id_type=MESH)

    def transfer(number, src, dst, device):
        return pltpu.make_async_remote_copy(
            src_ref=src,
            dst_ref=dst,
            send_sem=send_sem.at[number],
            recv_sem=recv_sem.at[number],
            device_id=device,
            device_id_type=MESH,
        )

    before, left, above = (sec - 1, tile), (sec, tile - 1), (sec, tile - GRID_COLS)
    below_main = [
        [
            transfer(
                4 * k + c,
                margins.at[k, 0, PATCH_ROWS + c, :, pl.ds(0, LANES)],
                main.at[BELOW + 4 * k + c],
                above,
            )
            for c in range(PATCH_COLS)
        ]
        for k in range(sections)
    ]
    below_rem = [transfer(8 + k, rem.at[9 + 1 + k], rem.at[7 + k], above) for k in range(sections)]
    left_main = [
        transfer(
            10 + 2 * k + r,
            margins.at[k, 0, r, :, pl.ds(0, LANES)],
            main.at[LEFT + 2 * k + r],
            left,
        )
        for k in range(sections)
        for r in range(PATCH_ROWS)
    ]
    left_rem = transfer(14, rem.at[9], rem.at[6], left)
    next_main = [
        transfer(
            15 + h,
            patches.at[0, 0, pl.ds(4 * h, 4), :, pl.ds(0, LANES)],
            main.at[pl.ds(NEXT + 4 * h, 4)],
            before,
        )
        for h in range(2)
    ]
    next_rem = [transfer(17 + h, rem.at[h], rem.at[4 + h], before) for h in range(2)]

    def start(copies):
        for copy in copies:
            copy.start()

    def pack(slot, sources):
        rem[slot] = jnp.concatenate([raw[i] for i in sources], axis=1)

    table_copy.wait()
    for copy in margin_raw:
        copy.wait()
    pack(10, [16 + PATCH_ROWS + c for c in range(4)])
    pack(11, [16 + EDGES + PATCH_ROWS + c for c in range(4)])
    pack(9, [16, 17, 16 + EDGES, 16 + EDGES + 1])

    greeted = functools.reduce(jnp.add, [there.astype(jnp.int32) for there, _ in peers])
    pl.semaphore_wait(barrier, greeted)

    @pl.when(has_above)
    def _():
        start(below_rem + below_main[0] + below_main[1])

    @pl.when(has_left)
    def _():
        start([left_rem] + left_main)

    @pl.when(has_before)
    def _():
        start(next_main)

    for copy in patch_raw:
        copy.wait()
    for h in range(4):
        pack(h, [4 * h + p for p in range(4)])

    @pl.when(has_before)
    def _():
        start(next_rem)

    for copy in patch_main:
        copy.wait()

    lane = iota((1, LANES), 1)
    group_of_lane = lane // TAIL

    def spectra(group):
        tail = rem[group].astype(jnp.float32)
        tail_sum = jnp.sum(tail, axis=0, keepdims=True)
        means = []
        for p in range(GROUP):
            sums = jnp.sum(main[GROUP * group + p].astype(jnp.float32), axis=0, keepdims=True)
            sums = sums + jnp.where(group_of_lane == p, tail_sum, 0.0)
            means.append(jnp.sum(sums, axis=1, keepdims=True) * (1.0 / (SIDE * SIDE)))

        def by_lane(values):
            out = jnp.broadcast_to(values[0], (1, LANES))
            for p in range(1, GROUP):
                out = jnp.where(group_of_lane == p, values[p], out)
            return out

        tail = tail - by_lane(means)
        tail_sum = jnp.sum(tail * tail, axis=0, keepdims=True)
        scales = []
        for p in range(GROUP):
            centred = main[GROUP * group + p].astype(jnp.float32) - means[p]
            sums = jnp.sum(centred * centred, axis=0, keepdims=True)
            sums = sums + jnp.where(group_of_lane == p, tail_sum, 0.0)
            variance = jnp.sum(sums, axis=1, keepdims=True) * (1.0 / (SIDE * SIDE))
            scales.append(1.0 / jnp.sqrt(variance + 1e-05))
        tail = (tail * by_lane(scales)).astype(jnp.bfloat16)
        for p in range(GROUP):
            image = GROUP * group + p
            head = ((main[image].astype(jnp.float32) - means[p]) * scales[p]).astype(jnp.bfloat16)
            normal = jnp.concatenate([head, tail], axis=1)
            rows = dot(normal, table[T_ROW + 256 * p : T_ROW + 256 * (p + 1)]).astype(jnp.bfloat16)
            both = dot(table[CS_ROW : CS_ROW + 2 * BAND, :SIDE], rows)
            cc, cs = both[:BAND, :LANES], both[:BAND, LANES:]
            sc, ss = both[BAND:, :LANES], both[BAND:, LANES:]
            spec[image, 0] = jnp.concatenate([cc - ss, cc + ss], axis=1).astype(jnp.bfloat16)
            spec[image, 1] = jnp.concatenate([-(sc + cs), sc - cs], axis=1).astype(jnp.bfloat16)

    shift_rows = iota((16, SIDE), 1)
    kind = iota((16, SIDE), 0)

    def displace(pair, source, target, centre_row, centre_col):
        a_re, a_im = spec[source, 0].astype(jnp.float32), spec[source, 1].astype(jnp.float32)
        b_re, b_im = spec[target, 0].astype(jnp.float32), spec[target, 1].astype(jnp.float32)
        cross_re = (a_re * b_re + a_im * b_im).astype(jnp.bfloat16)
        cross_im = (a_im * b_re - a_re * b_im).astype(jnp.bfloat16)
        from_re = dot(cross_re, table[WRE_ROW : WRE_ROW + 256])
        from_im = dot(cross_im, table[WIM_ROW : WIM_ROW + 256])
        u_re, v_re = from_re[:, :LANES], from_re[:, LANES:]
        u_im, v_im = from_im[:, :LANES], from_im[:, LANES:]
        back_u = jnp.concatenate([u_re - u_im, u_re + u_im], axis=1).astype(jnp.bfloat16)
        back_v = jnp.concatenate([v_im + v_re, v_im - v_re], axis=1).astype(jnp.bfloat16)
        scores = dot(
            table[BACK_ROW : BACK_ROW + SIDE, : 2 * BAND],
            jnp.concatenate([back_u, back_v], axis=0),
        )
        largest = jnp.max(scores, axis=0, keepdims=True)
        weights = jnp.exp2((scores - largest) * EXP2_SCALE).astype(jnp.bfloat16)
        labels = wrapped(shift_rows, centre_row)
        labels = jnp.where(kind == 0, 1.0, jnp.where(kind == 1, labels, 0.0)).astype(jnp.bfloat16)
        sums = dot(labels, weights)
        peak[pl.ds(pair, 1), :] = largest
        total[pl.ds(pair, 1), :] = sums[0:1]
        moment[pl.ds(pair, 1), :] = sums[1:2]
        centre[pl.ds(pair, 1), :] = jnp.broadcast_to(centre_col, (1, 256))

    def displacements(first, count):
        wide = iota((count, 256), 1)
        near = wide < LANES
        shift = jnp.where(near, wide, SIDE + LANES - wide)
        valid = (near & (wide <= HALF)) | ((wide > LANES) & (wide < LANES + HALF))
        height = jnp.where(valid, peak[first : first + count], -jnp.inf)
        top = jnp.max(height, axis=1, keepdims=True)
        share = jnp.exp2((height - top) * EXP2_SCALE)
        share = jnp.where(valid, share, 0.0)
        mass = share * total[first : first + count]
        whole = jnp.sum(mass, axis=1, keepdims=True)
        labels = wrapped(shift, centre[first : first + count])
        scale = 1.0 / (whole * PIXEL_UNIT)
        rows = jnp.sum(share * moment[first : first + count], axis=1, keepdims=True) * scale
        cols = jnp.sum(mass * labels, axis=1, keepdims=True) * scale
        return rows, cols

    mesh_lane = iota((16, LANES), 1)
    mesh_row = iota((16, LANES), 0)
    mesh_peers = (
        (has_right, has_left, (sec, tile + 1)),
        (has_left, has_right, (sec, tile - 1)),
        (has_below, has_above, (sec, tile + GRID_COLS)),
        (has_above, has_below, (sec, tile - GRID_COLS)),
    )
    mesh_copies = [
        pltpu.make_async_remote_copy(
            src_ref=mesh_own,
            dst_ref=mesh_in.at[i],
            send_sem=mesh_send.at[i],
            recv_sem=mesh_recv.at[i],
            device_id=device,
            device_id_type=MESH,
        )
        for i, (_, _, device) in enumerate(mesh_peers)
    ]

    def send_mesh():
        rows, cols = displacements(0, 16)
        held = jnp.where(mesh_row < SLOTS, counts[0, 0], counts[0, sections - 1])
        last = jnp.where(has_after, 2 * SLOTS, SLOTS)
        usable = ((mesh_row & (SLOTS - 1)) < held) & (mesh_row < last)
        values = jnp.where(mesh_lane == 0, rows, jnp.where(mesh_lane == 1, cols, 1.0))
        mesh_own[...] = jnp.where(usable & (mesh_lane < 3), values, 0.0)
        for copy, (there, _, _) in zip(mesh_copies, mesh_peers):

            @pl.when(there)
            def _(copy=copy):
                copy.start()

    def smooth():
        for i, (copy, (_, comes, _)) in enumerate(zip(mesh_copies, mesh_peers)):

            @pl.when(comes)
            def _(copy=copy):
                copy.wait_recv()

            @pl.when(jnp.logical_not(comes))
            def _(i=i):
                mesh_in[i] = jnp.zeros((16, LANES), jnp.float32)

        beside = []
        for k in range(sections):
            for r in range(PATCH_ROWS):
                for c in range(PATCH_COLS):
                    base = SLOTS * k

                    def at(ref, row, col, base=base):
                        q = base + PATCH_COLS * row + col
                        return ref[q : q + 1]

                    own = mesh_own
                    parts = [
                        at(own, r, c - 1) if c > 0 else at(mesh_in.at[0], r, PATCH_COLS - 1),
                        at(own, r, c + 1) if c < PATCH_COLS - 1 else at(mesh_in.at[1], r, 0),
                        at(own, r - 1, c) if r > 0 else at(mesh_in.at[2], PATCH_ROWS - 1, c),
                        at(own, r + 1, c) if r < PATCH_ROWS - 1 else at(mesh_in.at[3], 0, c),
                    ]
                    beside.append(functools.reduce(jnp.add, parts))
        beside = jnp.concatenate(beside, axis=0)
        own = mesh_own[...]
        value = own[:, 2:3] * (2.0 * own + beside) / (2.0 + beside[:, 2:3])
        for k in range(sections):
            for axis in range(2):
                diagonal = jnp.where(mesh_row == mesh_lane + SLOTS * k, value[:, axis : axis + 1], 0.0)
                flow_out[k, 0, axis : axis + 1, :] = jnp.sum(diagonal, axis=0, keepdims=True)[:, :SLOTS]

    def finish_seams():
        rows, cols = displacements(16, 16)
        row, where = iota((16, LANES), 0), iota((16, LANES), 1)
        usable = ((row < 4) & has_right) | ((row >= 4) & has_below)
        for k in range(sections):
            pick = jnp.where(where < PATCH_ROWS, 2 * k + where, 4 + 4 * k + where - PATCH_ROWS)
            pick = (row == pick) & usable
            for axis, value in enumerate((rows, cols)):
                seam = jnp.sum(jnp.where(pick, value, 0.0), axis=0, keepdims=True)
                seams_out[k, 0, axis : axis + 1, :] = seam[:, :EDGES]

    def own_spectra(group, carry):
        spectra(group)
        return carry

    lax.fori_loop(0, 2, own_spectra, 0)

    def stage(i, carry):
        @pl.when((i == 2) & has_after)
        def _():
            next_rem[0].wait_recv()
            next_main[0].wait_recv()

        @pl.when((i == 3) & has_after)
        def _():
            next_rem[1].wait_recv()
            next_main[1].wait_recv()

        @pl.when(i == 4)
        def _():
            send_mesh()

        @pl.when((i == 4) & has_right)
        def _():
            left_rem.wait_recv()
            for copy in left_main:
                copy.wait_recv()

        @pl.when((i == 5) & has_below)
        def _():
            below_rem[0].wait_recv()
            for copy in below_main[0]:
                copy.wait_recv()

        @pl.when(i == 6)
        def _():
            smooth()

        @pl.when((i == 6) & has_below)
        def _():
            below_rem[1].wait_recv()
            for copy in below_main[1]:
                copy.wait_recv()

        there = (
            (i < 2)
            | ((i < 4) & has_after)
            | ((i == 4) & has_right)
            | ((i > 4) & has_below)
        )

        @pl.when(there)
        def _():
            spectra(i + 2)
            for p in range(GROUP):
                pair = GROUP * i + p
                cross = i < 4
                left_source = SLOTS * (p // 2) + PATCH_COLS * (p % 2) + PATCH_COLS - 1
                below_source = SLOTS * (i - 5) + PATCH_COLS + p
                source = jnp.where(cross, pair, jnp.where(i == 4, left_source, below_source))
                section = jnp.where(cross, i // 2, 0)
                slot = jnp.where(cross, lax.rem(i, 2) * GROUP + p, 0)
                centre_row = jnp.where(cross, offsets[section, 0, 0, slot], 0)
                centre_col = jnp.where(cross, offsets[section, 0, 1, slot], 0)
                displace(pair, source, SLOTS + pair, centre_row, centre_col)

        return carry

    lax.fori_loop(0, 7, stage, 0)
    finish_seams()

    def drain(copies):
        for copy in copies:
            copy.wait_send()

    @pl.when(has_above)
    def _():
        drain(below_rem + below_main[0] + below_main[1])

    @pl.when(has_left)
    def _():
        drain([left_rem] + left_main)

    @pl.when(has_before)
    def _():
        drain(next_main + next_rem)

    for copy, (there, _, _) in zip(mesh_copies, mesh_peers):

        @pl.when(there)
        def _(copy=copy):
            copy.wait_send()


def local(patches, margins, offsets, counts):
    sections = patches.shape[0]
    hbm = pl.BlockSpec(memory_space=pltpu.HBM)
    smem = pl.BlockSpec(memory_space=pltpu.SMEM)
    vmem = pl.BlockSpec(memory_space=pltpu.VMEM)
    bf16, f32 = jnp.bfloat16, jnp.float32
    return tuple(
        pl.pallas_call(
            functools.partial(kernel, sections),
            out_shape=(
                jax.ShapeDtypeStruct((sections, 1, 2, SLOTS), f32),
                jax.ShapeDtypeStruct((sections, 1, 2, EDGES), f32),
            ),
            in_specs=[hbm, hbm, hbm, smem, smem],
            out_specs=(vmem, vmem),
            scratch_shapes=[
                pltpu.VMEM((TABLE_ROWS, 256), bf16),
                pltpu.VMEM((IMAGES, SIDE, LANES), bf16),
                pltpu.VMEM((12, SIDE, LANES), bf16),
                pltpu.VMEM((28, SIDE, TAIL), bf16),
                pltpu.VMEM((IMAGES, 2, BAND, 256), bf16),
                pltpu.VMEM((PAIR_ROWS, 256), f32),
                pltpu.VMEM((PAIR_ROWS, 256), f32),
                pltpu.VMEM((PAIR_ROWS, 256), f32),
                pltpu.VMEM((PAIR_ROWS, 256), jnp.int32),
                pltpu.VMEM((16, LANES), f32),
                pltpu.VMEM((4, 16, LANES), f32),
                pltpu.SemaphoreType.DMA((8,)),
                pltpu.SemaphoreType.DMA((19,)),
                pltpu.SemaphoreType.DMA((19,)),
                pltpu.SemaphoreType.DMA((4,)),
                pltpu.SemaphoreType.DMA((4,)),
            ],
            compiler_params=pltpu.CompilerParams(
                collective_id=0, has_side_effects=True, vmem_limit_bytes=60 * 1024 * 1024
            ),
        )(patches, margins, jnp.asarray(tables()), jnp.swapaxes(offsets, 2, 3), jnp.swapaxes(counts, 0, 1))
    )


def solution(mesh):
    return jax.shard_map(
        local,
        mesh=mesh,
        in_specs=(
            P("sec", "xy", None, None, None),
            P("sec", "xy", None, None, None),
            P("sec", "xy", None, None),
            P("sec", "xy"),
        ),
        out_specs=(P("sec", "xy", None, None), P("sec", "xy", None, None)),
        check_vma=False,
    )
```

```python
import functools

import jax
import jax.numpy as jnp
import ml_dtypes
import numpy as np
from jax import lax
from jax.experimental import pallas as pl
from jax.experimental.pallas import tpu as pltpu
from jax.sharding import PartitionSpec as P

SIDE = 160
HALF = SIDE // 2
PATCH_ROWS = 2
PATCH_COLS = 4
GRID_COLS = 4
SLOTS = PATCH_ROWS * PATCH_COLS
EDGES = PATCH_ROWS + PATCH_COLS
LANES = 128
TAIL = SIDE - LANES
GROUP = 4
BAND = 96
PIXEL_UNIT = 16.0
LOG2E = 1.4426950408889634
SCORE_SCALE = 2.0 / float(SIDE) ** 3
EXP2_SCALE = SCORE_SCALE * LOG2E

T_ROW = 0
WRE_ROW = T_ROW + 256
WIM_ROW = WRE_ROW + 256
CS_ROW = WIM_ROW + 256
BACK_ROW = CS_ROW + 2 * BAND
TABLE_ROWS = BACK_ROW + SIDE

NEXT = 16
LEFT = 24
BELOW = 28
IMAGES = 36
PAIRS = 28
PAIR_ROWS = 32

MESH = pl.DeviceIdType.MESH


def tables():
    freq = np.arange(SIDE)
    phase = (freq[:, None] * freq[None, :]) % SIDE
    angle = phase.astype(np.float32) * np.float32(2.0 * np.pi / SIDE)
    cosine = np.cos(angle).astype(ml_dtypes.bfloat16).astype(np.float32)
    sine = np.sin(angle).astype(ml_dtypes.bfloat16).astype(np.float32)
    n = HALF + 1
    out = np.zeros((TABLE_ROWS, 256), np.float32)
    right = np.zeros((SIDE, 256), np.float32)
    right[:, :n] = cosine[:, :n]
    right[:, 128 : 128 + n] = sine[:, :n]
    out[T_ROW : T_ROW + SIDE] = right
    inner = np.ones((n, 1), np.float32)
    inner[0] = inner[HALF] = 0.0
    cos_half, sin_half = cosine[:n, :n], sine[:n, :n]
    out[WRE_ROW : WRE_ROW + n, :n] = cos_half
    out[WRE_ROW + 128 : WRE_ROW + 128 + n, :n] = cos_half * inner
    out[WRE_ROW : WRE_ROW + n, 128 : 128 + n] = sin_half
    out[WRE_ROW + 128 : WRE_ROW + 128 + n, 128 : 128 + n] = -sin_half * inner
    out[WIM_ROW : WIM_ROW + n, :n] = sin_half
    out[WIM_ROW + 128 : WIM_ROW + 128 + n, :n] = sin_half * inner
    out[WIM_ROW : WIM_ROW + n, 128 : 128 + n] = cos_half
    out[WIM_ROW + 128 : WIM_ROW + 128 + n, 128 : 128 + n] = -cos_half * inner
    out[CS_ROW : CS_ROW + n, :SIDE] = cosine[:n]
    out[CS_ROW + BAND : CS_ROW + BAND + n, :SIDE] = sine[:n]
    twice = 1.0 + inner[:, 0]
    out[BACK_ROW : BACK_ROW + SIDE, :n] = cosine[:, :n] * twice
    out[BACK_ROW : BACK_ROW + SIDE, BAND : BAND + n] = -sine[:, :n] * twice
    return out.astype(ml_dtypes.bfloat16)


def iota(shape, axis):
    return lax.broadcasted_iota(jnp.int32, shape, axis)


def dot(a, b):
    return jnp.dot(a, b, preferred_element_type=jnp.float32)


def wrapped(index, centre):
    return jnp.where(index >= centre + HALF, index - SIDE, index).astype(jnp.float32)


def kernel(
    sections,
    patches,
    margins,
    table_in,
    offsets_in,
    counts_in,
    flow_out,
    seams_out,
    offsets,
    counts,
    table,
    main,
    rem,
    raw,
    spec,
    peak,
    total,
    moment,
    centre,
    mesh_own,
    mesh_in,
    local_sem,
    send_sem,
    recv_sem,
    mesh_send,
    mesh_recv,
    ready,
):
    sec = lax.axis_index("sec")
    tile = lax.axis_index("xy")
    sec_total = lax.axis_size("sec")
    tile_total = lax.axis_size("xy")
    column = lax.rem(tile, GRID_COLS)
    has_before = sec > 0
    has_after = sec < sec_total - 1
    has_left = column > 0
    has_right = column < GRID_COLS - 1
    has_above = tile >= GRID_COLS
    has_below = tile < tile_total - GRID_COLS
    place = lax.rem(tile, 2 * GRID_COLS)
    host = place >= GRID_COLS
    guest = jnp.logical_not(host)
    first_turn = (place & 2) == 0
    second_turn = jnp.logical_not(first_turn)

    barrier = pltpu.get_barrier_semaphore()
    beside = (
        (has_before, (sec - 1, tile)),
        (has_after, (sec + 1, tile)),
        (has_left, (sec, tile - 1)),
        (has_right, (sec, tile + 1)),
    )
    across = (
        (has_above, (sec, tile - GRID_COLS), 1),
        (has_below, (sec, tile + GRID_COLS), 0),
    )
    for there, device in beside:

        @pl.when(there)
        def _(device=device):
            pl.semaphore_signal(barrier, inc=1, device_id=device, device_id_type=MESH)

    for there, device, _ in across:

        @pl.when(there & guest)
        def _(device=device):
            pl.semaphore_signal(barrier, inc=1, device_id=device, device_id_type=MESH)

    local_copies = []

    def fetch(src, dst):
        copy = pltpu.make_async_copy(src, dst, local_sem.at[len(local_copies)])
        copy.start()
        local_copies.append(copy)
        return copy

    margin_raw = [
        fetch(margins.at[k, 0, :, :, pl.ds(LANES, TAIL)], raw.at[pl.ds(16 + EDGES * k, EDGES)])
        for k in range(sections)
    ]
    patch_raw = [
        fetch(patches.at[k, 0, :, :, pl.ds(LANES, TAIL)], raw.at[pl.ds(SLOTS * k, SLOTS)])
        for k in range(sections)
    ]
    patch_main = [
        fetch(patches.at[k, 0, :, :, pl.ds(0, LANES)], main.at[pl.ds(SLOTS * k, SLOTS)])
        for k in range(sections)
    ]
    rest = [fetch(table_in, table), fetch(offsets_in, offsets), fetch(counts_in, counts)]

    def transfer(number, src, dst, device):
        return pltpu.make_async_remote_copy(
            src_ref=src,
            dst_ref=dst,
            send_sem=send_sem.at[number],
            recv_sem=recv_sem.at[number],
            device_id=device,
            device_id_type=MESH,
        )

    before, left, above = (sec - 1, tile), (sec, tile - 1), (sec, tile - GRID_COLS)
    below_main = [
        [
            transfer(
                4 * k + c,
                margins.at[k, 0, PATCH_ROWS + c, :, pl.ds(0, LANES)],
                main.at[BELOW + 4 * k + c],
                above,
            )
            for c in range(PATCH_COLS)
        ]
        for k in range(sections)
    ]
    below_rem = [transfer(8 + k, rem.at[9 + 1 + k], rem.at[7 + k], above) for k in range(sections)]
    left_main = [
        transfer(
            10 + 2 * k + r,
            margins.at[k, 0, r, :, pl.ds(0, LANES)],
            main.at[LEFT + 2 * k + r],
            left,
        )
        for k in range(sections)
        for r in range(PATCH_ROWS)
    ]
    left_rem = transfer(14, rem.at[9], rem.at[6], left)
    next_main = [
        transfer(
            15 + h,
            patches.at[0, 0, pl.ds(4 * h, 4), :, pl.ds(0, LANES)],
            main.at[pl.ds(NEXT + 4 * h, 4)],
            before,
        )
        for h in range(2)
    ]
    next_rem = [transfer(17 + h, rem.at[h], rem.at[4 + h], before) for h in range(2)]

    def start(copies):
        for copy in copies:
            copy.start()

    def pack(slot, sources):
        rem[slot] = jnp.concatenate([raw[i] for i in sources], axis=1)

    greeted = functools.reduce(jnp.add, [there.astype(jnp.int32) for there, _ in beside])
    greeted += functools.reduce(jnp.add, [(there & host).astype(jnp.int32) for there, _, _ in across])
    pl.semaphore_wait(barrier, greeted)
    for there, device, side in across:

        @pl.when(there & host)
        def _(device=device, side=side):
            pl.semaphore_signal(ready.at[side], inc=1, device_id=device, device_id_type=MESH)

    @pl.when(has_left)
    def _():
        start(left_main)

    @pl.when(has_above & host & first_turn)
    def _():
        start(below_main[0])

    @pl.when(has_before)
    def _():
        start(next_main)

    for copy in margin_raw:
        copy.wait()
    pack(9, [16, 17, 16 + EDGES, 16 + EDGES + 1])
    pack(10, [16 + PATCH_ROWS + c for c in range(4)])
    pack(11, [16 + EDGES + PATCH_ROWS + c for c in range(4)])

    @pl.when(has_left)
    def _():
        start([left_rem])

    @pl.when(has_above & host & first_turn)
    def _():
        start([below_rem[0], below_rem[1]] + below_main[1])

    for copy in patch_raw:
        copy.wait()
    for h in range(4):
        pack(h, [4 * h + p for p in range(4)])

    @pl.when(has_before)
    def _():
        start(next_rem)

    for copy in patch_main + rest:
        copy.wait()

    def start_below():
        start([below_rem[0]] + below_main[0] + [below_rem[1]] + below_main[1])

    lane = iota((1, LANES), 1)
    group_of_lane = lane // TAIL

    def spectra(group):
        tail = rem[group].astype(jnp.float32)
        tail_sum = jnp.sum(tail, axis=0, keepdims=True)
        means = []
        for p in range(GROUP):
            sums = jnp.sum(main[GROUP * group + p].astype(jnp.float32), axis=0, keepdims=True)
            sums = sums + jnp.where(group_of_lane == p, tail_sum, 0.0)
            means.append(jnp.sum(sums, axis=1, keepdims=True) * (1.0 / (SIDE * SIDE)))

        def by_lane(values):
            out = jnp.broadcast_to(values[0], (1, LANES))
            for p in range(1, GROUP):
                out = jnp.where(group_of_lane == p, values[p], out)
            return out

        tail = tail - by_lane(means)
        tail_sum = jnp.sum(tail * tail, axis=0, keepdims=True)
        scales = []
        for p in range(GROUP):
            centred = main[GROUP * group + p].astype(jnp.float32) - means[p]
            sums = jnp.sum(centred * centred, axis=0, keepdims=True)
            sums = sums + jnp.where(group_of_lane == p, tail_sum, 0.0)
            variance = jnp.sum(sums, axis=1, keepdims=True) * (1.0 / (SIDE * SIDE))
            scales.append(1.0 / jnp.sqrt(variance + 1e-05))
        tail = tail * by_lane(scales)
        normal = []
        for p in range(GROUP):
            head = (main[GROUP * group + p].astype(jnp.float32) - means[p]) * scales[p]
            rolled = tail if p == 0 else pltpu.roll(tail, LANES - TAIL * p, 1)
            normal.append(jnp.concatenate([head, rolled], axis=1).astype(jnp.bfloat16))
        normal = jnp.concatenate(normal, axis=0)
        rows = dot(normal, table[T_ROW : T_ROW + 256]).astype(jnp.bfloat16)
        for p in range(GROUP):
            image = GROUP * group + p
            both = dot(table[CS_ROW : CS_ROW + 2 * BAND, :SIDE], rows[SIDE * p : SIDE * (p + 1)])
            cc, cs = both[:BAND, :LANES], both[:BAND, LANES:]
            sc, ss = both[BAND:, :LANES], both[BAND:, LANES:]
            spec[image, 0] = jnp.concatenate([cc - ss, cc + ss], axis=1).astype(jnp.bfloat16)
            spec[image, 1] = jnp.concatenate([-(sc + cs), sc - cs], axis=1).astype(jnp.bfloat16)

    shift_rows = iota((SIDE, LANES), 0)

    def displace(items):
        cross_re, cross_im = [], []
        for _, source, target, _, _ in items:
            a_re, a_im = spec[source, 0].astype(jnp.float32), spec[source, 1].astype(jnp.float32)
            b_re, b_im = spec[target, 0].astype(jnp.float32), spec[target, 1].astype(jnp.float32)
            cross_re.append((a_re * b_re + a_im * b_im).astype(jnp.bfloat16))
            cross_im.append((a_im * b_re - a_re * b_im).astype(jnp.bfloat16))
        all_re = dot(jnp.concatenate(cross_re, axis=0), table[WRE_ROW : WRE_ROW + 256])
        all_im = dot(jnp.concatenate(cross_im, axis=0), table[WIM_ROW : WIM_ROW + 256])
        for p, (pair, _, _, centre_row, centre_col) in enumerate(items):
            from_re, from_im = all_re[BAND * p : BAND * (p + 1)], all_im[BAND * p : BAND * (p + 1)]
            u_re, v_re = from_re[:, :LANES], from_re[:, LANES:]
            u_im, v_im = from_im[:, :LANES], from_im[:, LANES:]
            back_u = jnp.concatenate([u_re - u_im, u_re + u_im], axis=1).astype(jnp.bfloat16)
            back_v = jnp.concatenate([v_im + v_re, v_im - v_re], axis=1).astype(jnp.bfloat16)
            scores = dot(
                table[BACK_ROW : BACK_ROW + SIDE, : 2 * BAND],
                jnp.concatenate([back_u, back_v], axis=0),
            )
            largest = jnp.max(scores, axis=0, keepdims=True)
            weights = jnp.exp2((scores - largest) * EXP2_SCALE)
            labels = wrapped(shift_rows, centre_row)
            labels = jnp.concatenate([labels, labels], axis=1)
            peak[pl.ds(pair, 1), :] = largest
            total[pl.ds(pair, 1), :] = jnp.sum(weights, axis=0, keepdims=True)
            moment[pl.ds(pair, 1), :] = jnp.sum(weights * labels, axis=0, keepdims=True)
            centre[pl.ds(pair, 1), :] = jnp.broadcast_to(centre_col, (1, 256))

    def displacements(first, count):
        wide = iota((count, 256), 1)
        near = wide < LANES
        shift = jnp.where(near, wide, SIDE + LANES - wide)
        valid = (near & (wide <= HALF)) | ((wide > LANES) & (wide < LANES + HALF))
        height = jnp.where(valid, peak[first : first + count], -jnp.inf)
        top = jnp.max(height, axis=1, keepdims=True)
        share = jnp.exp2((height - top) * EXP2_SCALE)
        share = jnp.where(valid, share, 0.0)
        mass = share * total[first : first + count]
        whole = jnp.sum(mass, axis=1, keepdims=True)
        labels = wrapped(shift, centre[first : first + count])
        scale = 1.0 / (whole * PIXEL_UNIT)
        rows = jnp.sum(share * moment[first : first + count], axis=1, keepdims=True) * scale
        cols = jnp.sum(mass * labels, axis=1, keepdims=True) * scale
        return rows, cols

    mesh_lane = iota((16, LANES), 1)
    mesh_row = iota((16, LANES), 0)
    mesh_peers = (
        (has_right, has_left, (sec, tile + 1)),
        (has_left, has_right, (sec, tile - 1)),
        (has_below, has_above, (sec, tile + GRID_COLS)),
        (has_above, has_below, (sec, tile - GRID_COLS)),
    )
    mesh_copies = [
        pltpu.make_async_remote_copy(
            src_ref=mesh_own,
            dst_ref=mesh_in.at[i],
            send_sem=mesh_send.at[i],
            recv_sem=mesh_recv.at[i],
            device_id=device,
            device_id_type=MESH,
        )
        for i, (_, _, device) in enumerate(mesh_peers)
    ]

    def send_mesh():
        rows, cols = displacements(0, 16)
        held = jnp.where(mesh_row < SLOTS, counts[0, 0], counts[0, sections - 1])
        last = jnp.where(has_after, 2 * SLOTS, SLOTS)
        usable = ((mesh_row & (SLOTS - 1)) < held) & (mesh_row < last)
        values = jnp.where(mesh_lane == 0, rows, jnp.where(mesh_lane == 1, cols, 1.0))
        mesh_own[...] = jnp.where(usable & (mesh_lane < 3), values, 0.0)
        for copy, (there, _, _) in zip(mesh_copies, mesh_peers):

            @pl.when(there)
            def _(copy=copy):
                copy.start()

    def smooth():
        for i, (copy, (_, comes, _)) in enumerate(zip(mesh_copies, mesh_peers)):

            @pl.when(comes)
            def _(copy=copy):
                copy.wait_recv()

            @pl.when(jnp.logical_not(comes))
            def _(i=i):
                mesh_in[i] = jnp.zeros((16, LANES), jnp.float32)

        beside = []
        for k in range(sections):
            for r in range(PATCH_ROWS):
                for c in range(PATCH_COLS):
                    base = SLOTS * k

                    def at(ref, row, col, base=base):
                        q = base + PATCH_COLS * row + col
                        return ref[q : q + 1]

                    own = mesh_own
                    parts = [
                        at(own, r, c - 1) if c > 0 else at(mesh_in.at[0], r, PATCH_COLS - 1),
                        at(own, r, c + 1) if c < PATCH_COLS - 1 else at(mesh_in.at[1], r, 0),
                        at(own, r - 1, c) if r > 0 else at(mesh_in.at[2], PATCH_ROWS - 1, c),
                        at(own, r + 1, c) if r < PATCH_ROWS - 1 else at(mesh_in.at[3], 0, c),
                    ]
                    beside.append(functools.reduce(jnp.add, parts))
        beside = jnp.concatenate(beside, axis=0)
        own = mesh_own[...]
        value = own[:, 2:3] * (2.0 * own + beside) / (2.0 + beside[:, 2:3])
        for k in range(sections):
            for axis in range(2):
                diagonal = jnp.where(mesh_row == mesh_lane + SLOTS * k, value[:, axis : axis + 1], 0.0)
                flow_out[k, 0, axis : axis + 1, :] = jnp.sum(diagonal, axis=0, keepdims=True)[:, :SLOTS]

    def finish_seams():
        rows, cols = displacements(16, 16)
        row, where = iota((16, LANES), 0), iota((16, LANES), 1)
        usable = ((row < 4) & has_right) | ((row >= 4) & has_below)
        for k in range(sections):
            pick = jnp.where(where < PATCH_ROWS, 2 * k + where, 4 + 4 * k + where - PATCH_ROWS)
            pick = (row == pick) & usable
            for axis, value in enumerate((rows, cols)):
                seam = jnp.sum(jnp.where(pick, value, 0.0), axis=0, keepdims=True)
                seams_out[k, 0, axis : axis + 1, :] = seam[:, :EDGES]

    def own_spectra(group, carry):
        spectra(group)
        return carry

    lax.fori_loop(0, 2, own_spectra, 0)

    def stage(i, carry):
        for there, _, side in across:

            @pl.when((i == 1) & there & guest)
            def _(side=side):
                pl.semaphore_wait(ready.at[1 - side], 1)

        @pl.when((i == 1) & has_above & guest & first_turn)
        def _():
            start_below()

        @pl.when((i == 2) & has_above & host & second_turn)
        def _():
            start_below()

        @pl.when((i == 4) & has_above & guest & second_turn)
        def _():
            start_below()

        @pl.when((i == 5) & has_below)
        def _():
            below_rem[0].wait_recv()

        @pl.when((i == 2) & has_after)
        def _():
            next_rem[0].wait_recv()
            next_main[0].wait_recv()

        @pl.when((i == 3) & has_after)
        def _():
            next_rem[1].wait_recv()
            next_main[1].wait_recv()

        @pl.when(i == 4)
        def _():
            send_mesh()

        @pl.when((i == 4) & has_right)
        def _():
            left_rem.wait_recv()
            for copy in left_main:
                copy.wait_recv()

        @pl.when((i == 5) & has_below)
        def _():
            for copy in below_main[0]:
                copy.wait_recv()

        @pl.when(i == 6)
        def _():
            smooth()

        @pl.when((i == 6) & has_below)
        def _():
            below_rem[1].wait_recv()
            for copy in below_main[1]:
                copy.wait_recv()

        there = (
            (i < 2)
            | ((i < 4) & has_after)
            | ((i == 4) & has_right)
            | ((i > 4) & has_below)
        )

        @pl.when(there)
        def _():
            spectra(i + 2)
            items = []
            for p in range(GROUP):
                pair = GROUP * i + p
                cross = i < 4
                left_source = SLOTS * (p // 2) + PATCH_COLS * (p % 2) + PATCH_COLS - 1
                below_source = SLOTS * (i - 5) + PATCH_COLS + p
                source = jnp.where(cross, pair, jnp.where(i == 4, left_source, below_source))
                section = jnp.where(cross, i // 2, 0)
                slot = jnp.where(cross, lax.rem(i, 2) * GROUP + p, 0)
                centre_row = jnp.where(cross, offsets[section, 0, 0, slot], 0)
                centre_col = jnp.where(cross, offsets[section, 0, 1, slot], 0)
                items.append((pair, source, SLOTS + pair, centre_row, centre_col))
            displace(items)

        return carry

    lax.fori_loop(0, 7, stage, 0)
    finish_seams()

    def drain(copies):
        for copy in copies:
            copy.wait_send()

    @pl.when(has_above)
    def _():
        drain(below_rem + below_main[0] + below_main[1])

    @pl.when(has_left)
    def _():
        drain([left_rem] + left_main)

    @pl.when(has_before)
    def _():
        drain(next_main + next_rem)

    for copy, (there, _, _) in zip(mesh_copies, mesh_peers):

        @pl.when(there)
        def _(copy=copy):
            copy.wait_send()


def local(patches, margins, offsets, counts):
    sections = patches.shape[0]
    hbm = pl.BlockSpec(memory_space=pltpu.HBM)
    vmem = pl.BlockSpec(memory_space=pltpu.VMEM)
    bf16, f32 = jnp.bfloat16, jnp.float32
    flow, seams = (
        pl.pallas_call(
            functools.partial(kernel, sections),
            out_shape=(
                jax.ShapeDtypeStruct((sections, 1, 2, SLOTS), f32),
                jax.ShapeDtypeStruct((sections, 1, 2, EDGES), f32),
            ),
            in_specs=[hbm] * 5,
            out_specs=(vmem, vmem),
            scratch_shapes=[
                pltpu.SMEM((sections, 1, 2, SLOTS), jnp.int32),
                pltpu.SMEM((1, sections), jnp.int32),
                pltpu.VMEM((TABLE_ROWS, 256), bf16),
                pltpu.VMEM((IMAGES, SIDE, LANES), bf16),
                pltpu.VMEM((12, SIDE, LANES), bf16),
                pltpu.VMEM((28, SIDE, TAIL), bf16),
                pltpu.VMEM((IMAGES, 2, BAND, 256), bf16),
                pltpu.VMEM((PAIR_ROWS, 256), f32),
                pltpu.VMEM((PAIR_ROWS, 256), f32),
                pltpu.VMEM((PAIR_ROWS, 256), f32),
                pltpu.VMEM((PAIR_ROWS, 256), jnp.int32),
                pltpu.VMEM((16, LANES), f32),
                pltpu.VMEM((4, 16, LANES), f32),
                pltpu.SemaphoreType.DMA((9,)),
                pltpu.SemaphoreType.DMA((19,)),
                pltpu.SemaphoreType.DMA((19,)),
                pltpu.SemaphoreType.DMA((4,)),
                pltpu.SemaphoreType.DMA((4,)),
                pltpu.SemaphoreType.REGULAR((2,)),
            ],
            compiler_params=pltpu.CompilerParams(
                collective_id=0, has_side_effects=True, vmem_limit_bytes=60 * 1024 * 1024
            ),
        )(patches, margins, jnp.asarray(tables()), jnp.swapaxes(offsets, 2, 3), jnp.swapaxes(counts, 0, 1))
    )
    return tuple(
        pl.pallas_call(
            hand_over,
            out_shape=(
                jax.ShapeDtypeStruct(flow.shape, f32),
                jax.ShapeDtypeStruct(seams.shape, f32),
            ),
            in_specs=[vmem, vmem],
            out_specs=(vmem, vmem),
        )(flow, seams)
    )


def hand_over(flow_in, seams_in, flow_out, seams_out):
    flow_out[...] = flow_in[...]
    seams_out[...] = seams_in[...]


def solution(mesh):
    return jax.shard_map(
        local,
        mesh=mesh,
        in_specs=(
            P("sec", "xy", None, None, None),
            P("sec", "xy", None, None, None),
            P("sec", "xy", None, None),
            P("sec", "xy"),
        ),
        out_specs=(P("sec", "xy", None, None), P("sec", "xy", None, None)),
        check_vma=False,
    )
```

```python
import functools

import jax
import jax.numpy as jnp
import ml_dtypes
import numpy as np
from jax import lax
from jax.experimental import pallas as pl
from jax.experimental.pallas import tpu as pltpu
from jax.sharding import PartitionSpec as P

SIDE = 160
HALF = SIDE // 2
PATCH_ROWS = 2
PATCH_COLS = 4
GRID_COLS = 4
SLOTS = PATCH_ROWS * PATCH_COLS
EDGES = PATCH_ROWS + PATCH_COLS
LANES = 128
TAIL = SIDE - LANES
GROUP = 4
BAND = 96
PIXEL_UNIT = 16.0
LOG2E = 1.4426950408889634
SCORE_SCALE = 2.0 / float(SIDE) ** 3
EXP2_SCALE = SCORE_SCALE * LOG2E

T_ROW = 0
WRE_ROW = T_ROW + 256
WIM_ROW = WRE_ROW + 256
CS_ROW = WIM_ROW + 256
BACK_ROW = CS_ROW + 2 * BAND
TABLE_ROWS = BACK_ROW + SIDE

NEXT = 16
LEFT = 24
BELOW = 28
IMAGES = 36
PAIRS = 28
PAIR_ROWS = 32

MESH = pl.DeviceIdType.MESH


def tables():
    freq = np.arange(SIDE)
    phase = (freq[:, None] * freq[None, :]) % SIDE
    angle = phase.astype(np.float32) * np.float32(2.0 * np.pi / SIDE)
    cosine = np.cos(angle).astype(ml_dtypes.bfloat16).astype(np.float32)
    sine = np.sin(angle).astype(ml_dtypes.bfloat16).astype(np.float32)
    n = HALF + 1
    out = np.zeros((TABLE_ROWS, 256), np.float32)
    right = np.zeros((SIDE, 256), np.float32)
    right[:, :n] = cosine[:, :n]
    right[:, 128 : 128 + n] = sine[:, :n]
    out[T_ROW : T_ROW + SIDE] = right
    inner = np.ones((n, 1), np.float32)
    inner[0] = inner[HALF] = 0.0
    cos_half, sin_half = cosine[:n, :n], sine[:n, :n]
    out[WRE_ROW : WRE_ROW + n, :n] = cos_half
    out[WRE_ROW + 128 : WRE_ROW + 128 + n, :n] = cos_half * inner
    out[WRE_ROW : WRE_ROW + n, 128 : 128 + n] = sin_half
    out[WRE_ROW + 128 : WRE_ROW + 128 + n, 128 : 128 + n] = -sin_half * inner
    out[WIM_ROW : WIM_ROW + n, :n] = sin_half
    out[WIM_ROW + 128 : WIM_ROW + 128 + n, :n] = sin_half * inner
    out[WIM_ROW : WIM_ROW + n, 128 : 128 + n] = cos_half
    out[WIM_ROW + 128 : WIM_ROW + 128 + n, 128 : 128 + n] = -cos_half * inner
    out[CS_ROW : CS_ROW + n, :SIDE] = cosine[:n]
    out[CS_ROW + BAND : CS_ROW + BAND + n, :SIDE] = sine[:n]
    twice = 1.0 + inner[:, 0]
    out[BACK_ROW : BACK_ROW + SIDE, :n] = cosine[:, :n] * twice
    out[BACK_ROW : BACK_ROW + SIDE, BAND : BAND + n] = -sine[:, :n] * twice
    return out.astype(ml_dtypes.bfloat16)


def iota(shape, axis):
    return lax.broadcasted_iota(jnp.int32, shape, axis)


def dot(a, b):
    return jnp.dot(a, b, preferred_element_type=jnp.float32)


def wrapped(index, centre):
    return jnp.where(index >= centre + HALF, index - SIDE, index).astype(jnp.float32)


def kernel(
    sections,
    patches,
    margins,
    table_in,
    offsets_in,
    counts_in,
    flow_out,
    seams_out,
    offsets,
    counts,
    table,
    main,
    rem,
    raw,
    spec,
    peak,
    total,
    moment,
    centre,
    mesh_own,
    mesh_in,
    local_sem,
    send_sem,
    recv_sem,
    mesh_send,
    mesh_recv,
    ready,
):
    sec = lax.axis_index("sec")
    tile = lax.axis_index("xy")
    sec_total = lax.axis_size("sec")
    tile_total = lax.axis_size("xy")
    column = lax.rem(tile, GRID_COLS)
    has_before = sec > 0
    has_after = sec < sec_total - 1
    has_left = column > 0
    has_right = column < GRID_COLS - 1
    has_above = tile >= GRID_COLS
    has_below = tile < tile_total - GRID_COLS
    place = lax.rem(tile, 2 * GRID_COLS)
    host = place >= GRID_COLS
    guest = jnp.logical_not(host)
    turns = (
        jnp.where(place == 0, 1, jnp.where(place == 1, 1, jnp.where(place == 2, 4, jnp.where(place == 3, 4, jnp.where(place == 4, -1, jnp.where(place == 5, -1, jnp.where(place == 6, 2, 2))))))),
        jnp.where(place == 0, 2, jnp.where(place == 1, 2, jnp.where(place == 2, 5, jnp.where(place == 3, 5, jnp.where(place == 4, -1, jnp.where(place == 5, -1, jnp.where(place == 6, 3, 3))))))),
    )

    barrier = pltpu.get_barrier_semaphore()
    beside = (
        (has_before, (sec - 1, tile)),
        (has_after, (sec + 1, tile)),
        (has_left, (sec, tile - 1)),
        (has_right, (sec, tile + 1)),
    )
    across = (
        (has_above, (sec, tile - GRID_COLS), 1),
        (has_below, (sec, tile + GRID_COLS), 0),
    )
    for there, device in beside:

        @pl.when(there)
        def _(device=device):
            pl.semaphore_signal(barrier, inc=1, device_id=device, device_id_type=MESH)

    for there, device, _ in across:

        @pl.when(there & guest)
        def _(device=device):
            pl.semaphore_signal(barrier, inc=1, device_id=device, device_id_type=MESH)

    def transfer(number, src, dst, device):
        return pltpu.make_async_remote_copy(
            src_ref=src,
            dst_ref=dst,
            send_sem=send_sem.at[number],
            recv_sem=recv_sem.at[number],
            device_id=device,
            device_id_type=MESH,
        )

    before, left, above = (sec - 1, tile), (sec, tile - 1), (sec, tile - GRID_COLS)
    below_main = [
        [
            transfer(
                4 * k + c,
                margins.at[k, 0, PATCH_ROWS + c, :, pl.ds(0, LANES)],
                main.at[BELOW + 4 * k + c],
                above,
            )
            for c in range(PATCH_COLS)
        ]
        for k in range(sections)
    ]
    below_rem = [transfer(8 + k, rem.at[9 + 1 + k], rem.at[7 + k], above) for k in range(sections)]
    left_main = [
        transfer(
            10 + 2 * k + r,
            margins.at[k, 0, r, :, pl.ds(0, LANES)],
            main.at[LEFT + 2 * k + r],
            left,
        )
        for k in range(sections)
        for r in range(PATCH_ROWS)
    ]
    left_rem = transfer(14, rem.at[9], rem.at[6], left)
    next_main = [
        transfer(
            15 + h,
            patches.at[0, 0, pl.ds(4 * h, 4), :, pl.ds(0, LANES)],
            main.at[pl.ds(NEXT + 4 * h, 4)],
            before,
        )
        for h in range(2)
    ]
    next_rem = [transfer(17 + h, rem.at[h], rem.at[4 + h], before) for h in range(2)]

    def start(copies):
        for copy in copies:
            copy.start()

    def pack(slot, sources):
        rem[slot] = jnp.concatenate([raw[i] for i in sources], axis=1)

    greeted = functools.reduce(jnp.add, [there.astype(jnp.int32) for there, _ in beside])
    greeted += functools.reduce(jnp.add, [(there & host).astype(jnp.int32) for there, _, _ in across])
    pl.semaphore_wait(barrier, greeted)
    for there, device, side in across:

        @pl.when(there & host)
        def _(device=device, side=side):
            pl.semaphore_signal(ready.at[side], inc=1, device_id=device, device_id_type=MESH)

    @pl.when(has_above & (turns[0] < 0))
    def _():
        start(below_main[0])

    @pl.when(has_left & guest)
    def _():
        start(left_main)

    @pl.when(has_before)
    def _():
        start(next_main)

    local_copies = []

    def fetch(src, dst):
        copy = pltpu.make_async_copy(src, dst, local_sem.at[len(local_copies)])
        copy.start()
        local_copies.append(copy)
        return copy

    margin_raw = [
        fetch(margins.at[k, 0, :, :, pl.ds(LANES, TAIL)], raw.at[pl.ds(16 + EDGES * k, EDGES)])
        for k in range(sections)
    ]
    patch_raw = [
        fetch(patches.at[k, 0, :, :, pl.ds(LANES, TAIL)], raw.at[pl.ds(SLOTS * k, SLOTS)])
        for k in range(sections)
    ]
    patch_main = [
        fetch(patches.at[k, 0, :, :, pl.ds(0, LANES)], main.at[pl.ds(SLOTS * k, SLOTS)])
        for k in range(sections)
    ]
    rest = [fetch(table_in, table), fetch(offsets_in, offsets), fetch(counts_in, counts)]

    for copy in margin_raw:
        copy.wait()
    pack(10, [16 + PATCH_ROWS + c for c in range(4)])
    pack(11, [16 + EDGES + PATCH_ROWS + c for c in range(4)])

    @pl.when(has_above & (turns[0] < 0))
    def _():
        start([below_rem[0]])

    @pl.when(has_above & (turns[1] < 0))
    def _():
        start([below_rem[1]] + below_main[1])

    pack(9, [16, 17, 16 + EDGES, 16 + EDGES + 1])

    @pl.when(has_left & guest)
    def _():
        start([left_rem])

    for copy in patch_raw:
        copy.wait()
    for h in range(4):
        pack(h, [4 * h + p for p in range(4)])

    @pl.when(has_before)
    def _():
        start(next_rem)

    for copy in patch_main + rest:
        copy.wait()

    lane = iota((1, LANES), 1)
    group_of_lane = lane // TAIL

    def spectra(group):
        tail = rem[group].astype(jnp.float32)
        tail_sum = jnp.sum(tail, axis=0, keepdims=True)
        means = []
        for p in range(GROUP):
            sums = jnp.sum(main[GROUP * group + p].astype(jnp.float32), axis=0, keepdims=True)
            sums = sums + jnp.where(group_of_lane == p, tail_sum, 0.0)
            means.append(jnp.sum(sums, axis=1, keepdims=True) * (1.0 / (SIDE * SIDE)))

        def by_lane(values):
            out = jnp.broadcast_to(values[0], (1, LANES))
            for p in range(1, GROUP):
                out = jnp.where(group_of_lane == p, values[p], out)
            return out

        tail = tail - by_lane(means)
        tail_sum = jnp.sum(tail * tail, axis=0, keepdims=True)
        scales = []
        for p in range(GROUP):
            centred = main[GROUP * group + p].astype(jnp.float32) - means[p]
            sums = jnp.sum(centred * centred, axis=0, keepdims=True)
            sums = sums + jnp.where(group_of_lane == p, tail_sum, 0.0)
            variance = jnp.sum(sums, axis=1, keepdims=True) * (1.0 / (SIDE * SIDE))
            scales.append(1.0 / jnp.sqrt(variance + 1e-05))
        tail = tail * by_lane(scales)
        normal = []
        for p in range(GROUP):
            head = (main[GROUP * group + p].astype(jnp.float32) - means[p]) * scales[p]
            rolled = tail if p == 0 else pltpu.roll(tail, LANES - TAIL * p, 1)
            normal.append(jnp.concatenate([head, rolled], axis=1).astype(jnp.bfloat16))
        normal = jnp.concatenate(normal, axis=0)
        rows = dot(normal, table[T_ROW : T_ROW + 256]).astype(jnp.bfloat16)
        for p in range(GROUP):
            image = GROUP * group + p
            both = dot(table[CS_ROW : CS_ROW + 2 * BAND, :SIDE], rows[SIDE * p : SIDE * (p + 1)])
            cc, cs = both[:BAND, :LANES], both[:BAND, LANES:]
            sc, ss = both[BAND:, :LANES], both[BAND:, LANES:]
            spec[image, 0] = jnp.concatenate([cc - ss, cc + ss], axis=1).astype(jnp.bfloat16)
            spec[image, 1] = jnp.concatenate([-(sc + cs), sc - cs], axis=1).astype(jnp.bfloat16)

    shift_rows = iota((SIDE, LANES), 0)

    def displace(items):
        cross_re, cross_im = [], []
        for _, source, target, _, _ in items:
            a_re, a_im = spec[source, 0].astype(jnp.float32), spec[source, 1].astype(jnp.float32)
            b_re, b_im = spec[target, 0].astype(jnp.float32), spec[target, 1].astype(jnp.float32)
            cross_re.append((a_re * b_re + a_im * b_im).astype(jnp.bfloat16))
            cross_im.append((a_im * b_re - a_re * b_im).astype(jnp.bfloat16))
        all_re = dot(jnp.concatenate(cross_re, axis=0), table[WRE_ROW : WRE_ROW + 256])
        all_im = dot(jnp.concatenate(cross_im, axis=0), table[WIM_ROW : WIM_ROW + 256])
        for p, (pair, _, _, centre_row, centre_col) in enumerate(items):
            from_re, from_im = all_re[BAND * p : BAND * (p + 1)], all_im[BAND * p : BAND * (p + 1)]
            u_re, v_re = from_re[:, :LANES], from_re[:, LANES:]
            u_im, v_im = from_im[:, :LANES], from_im[:, LANES:]
            back_u = jnp.concatenate([u_re - u_im, u_re + u_im], axis=1).astype(jnp.bfloat16)
            back_v = jnp.concatenate([v_im + v_re, v_im - v_re], axis=1).astype(jnp.bfloat16)
            scores = dot(
                table[BACK_ROW : BACK_ROW + SIDE, : 2 * BAND],
                jnp.concatenate([back_u, back_v], axis=0),
            )
            largest = jnp.max(scores, axis=0, keepdims=True)
            weights = jnp.exp2((scores - largest) * EXP2_SCALE)
            labels = wrapped(shift_rows, centre_row)
            labels = jnp.concatenate([labels, labels], axis=1)
            peak[pl.ds(pair, 1), :] = largest
            total[pl.ds(pair, 1), :] = jnp.sum(weights, axis=0, keepdims=True)
            moment[pl.ds(pair, 1), :] = jnp.sum(weights * labels, axis=0, keepdims=True)
            centre[pl.ds(pair, 1), :] = jnp.broadcast_to(centre_col, (1, 256))

    def displacements(first, count):
        wide = iota((count, 256), 1)
        near = wide < LANES
        shift = jnp.where(near, wide, SIDE + LANES - wide)
        valid = (near & (wide <= HALF)) | ((wide > LANES) & (wide < LANES + HALF))
        height = jnp.where(valid, peak[first : first + count], -jnp.inf)
        top = jnp.max(height, axis=1, keepdims=True)
        share = jnp.exp2((height - top) * EXP2_SCALE)
        share = jnp.where(valid, share, 0.0)
        mass = share * total[first : first + count]
        whole = jnp.sum(mass, axis=1, keepdims=True)
        labels = wrapped(shift, centre[first : first + count])
        scale = 1.0 / (whole * PIXEL_UNIT)
        rows = jnp.sum(share * moment[first : first + count], axis=1, keepdims=True) * scale
        cols = jnp.sum(mass * labels, axis=1, keepdims=True) * scale
        return rows, cols

    mesh_lane = iota((16, LANES), 1)
    mesh_row = iota((16, LANES), 0)
    mesh_peers = (
        (has_right, has_left, (sec, tile + 1)),
        (has_left, has_right, (sec, tile - 1)),
        (has_below, has_above, (sec, tile + GRID_COLS)),
        (has_above, has_below, (sec, tile - GRID_COLS)),
    )
    mesh_copies = [
        pltpu.make_async_remote_copy(
            src_ref=mesh_own,
            dst_ref=mesh_in.at[i],
            send_sem=mesh_send.at[i],
            recv_sem=mesh_recv.at[i],
            device_id=device,
            device_id_type=MESH,
        )
        for i, (_, _, device) in enumerate(mesh_peers)
    ]

    def send_mesh():
        rows, cols = displacements(0, 16)
        held = jnp.where(mesh_row < SLOTS, counts[0, 0], counts[0, sections - 1])
        last = jnp.where(has_after, 2 * SLOTS, SLOTS)
        usable = ((mesh_row & (SLOTS - 1)) < held) & (mesh_row < last)
        values = jnp.where(mesh_lane == 0, rows, jnp.where(mesh_lane == 1, cols, 1.0))
        mesh_own[...] = jnp.where(usable & (mesh_lane < 3), values, 0.0)
        for copy, (there, _, _) in zip(mesh_copies, mesh_peers):

            @pl.when(there)
            def _(copy=copy):
                copy.start()

    def smooth():
        for i, (copy, (_, comes, _)) in enumerate(zip(mesh_copies, mesh_peers)):

            @pl.when(comes)
            def _(copy=copy):
                copy.wait_recv()

            @pl.when(jnp.logical_not(comes))
            def _(i=i):
                mesh_in[i] = jnp.zeros((16, LANES), jnp.float32)

        beside = []
        for k in range(sections):
            for r in range(PATCH_ROWS):
                for c in range(PATCH_COLS):
                    base = SLOTS * k

                    def at(ref, row, col, base=base):
                        q = base + PATCH_COLS * row + col
                        return ref[q : q + 1]

                    own = mesh_own
                    parts = [
                        at(own, r, c - 1) if c > 0 else at(mesh_in.at[0], r, PATCH_COLS - 1),
                        at(own, r, c + 1) if c < PATCH_COLS - 1 else at(mesh_in.at[1], r, 0),
                        at(own, r - 1, c) if r > 0 else at(mesh_in.at[2], PATCH_ROWS - 1, c),
                        at(own, r + 1, c) if r < PATCH_ROWS - 1 else at(mesh_in.at[3], 0, c),
                    ]
                    beside.append(functools.reduce(jnp.add, parts))
        beside = jnp.concatenate(beside, axis=0)
        own = mesh_own[...]
        value = own[:, 2:3] * (2.0 * own + beside) / (2.0 + beside[:, 2:3])
        for k in range(sections):
            for axis in range(2):
                diagonal = jnp.where(mesh_row == mesh_lane + SLOTS * k, value[:, axis : axis + 1], 0.0)
                flow_out[k, 0, axis : axis + 1, :] = jnp.sum(diagonal, axis=0, keepdims=True)[:, :SLOTS]

    def finish_seams():
        rows, cols = displacements(16, 16)
        row, where = iota((16, LANES), 0), iota((16, LANES), 1)
        usable = ((row < 4) & has_right) | ((row >= 4) & has_below)
        for k in range(sections):
            pick = jnp.where(where < PATCH_ROWS, 2 * k + where, 4 + 4 * k + where - PATCH_ROWS)
            pick = (row == pick) & usable
            for axis, value in enumerate((rows, cols)):
                seam = jnp.sum(jnp.where(pick, value, 0.0), axis=0, keepdims=True)
                seams_out[k, 0, axis : axis + 1, :] = seam[:, :EDGES]

    def own_spectra(group, carry):
        spectra(group)
        return carry

    lax.fori_loop(0, 2, own_spectra, 0)

    def stage(step, carry):
        late = jnp.where(step == 6, 4, step + 1)
        i = jnp.where(host & (step >= 4), late, step)

        for there, _, side in across:

            @pl.when((step == 1) & there & guest)
            def _(side=side):
                pl.semaphore_wait(ready.at[1 - side], 1)

        for k in range(sections):

            @pl.when(has_above & (step == turns[k]))
            def _(k=k):
                start([below_rem[k]] + below_main[k])

        @pl.when(has_left & host & (step == 5))
        def _():
            start([left_rem] + left_main)

        @pl.when((i == 2) & has_after)
        def _():
            next_rem[0].wait_recv()
            next_main[0].wait_recv()

        @pl.when((i == 3) & has_after)
        def _():
            next_rem[1].wait_recv()
            next_main[1].wait_recv()

        @pl.when(step == 4)
        def _():
            send_mesh()

        @pl.when((i == 4) & has_right)
        def _():
            left_rem.wait_recv()
            for copy in left_main:
                copy.wait_recv()

        @pl.when((i == 5) & has_below)
        def _():
            below_rem[0].wait_recv()
            for copy in below_main[0]:
                copy.wait_recv()

        @pl.when(step == 6)
        def _():
            smooth()

        @pl.when((i == 6) & has_below)
        def _():
            below_rem[1].wait_recv()
            for copy in below_main[1]:
                copy.wait_recv()

        there = (
            (i < 2)
            | ((i < 4) & has_after)
            | ((i == 4) & has_right)
            | ((i > 4) & has_below)
        )

        @pl.when(there)
        def _():
            spectra(i + 2)
            items = []
            for p in range(GROUP):
                pair = GROUP * i + p
                cross = i < 4
                left_source = SLOTS * (p // 2) + PATCH_COLS * (p % 2) + PATCH_COLS - 1
                below_source = SLOTS * (i - 5) + PATCH_COLS + p
                source = jnp.where(cross, pair, jnp.where(i == 4, left_source, below_source))
                section = jnp.where(cross, i // 2, 0)
                slot = jnp.where(cross, lax.rem(i, 2) * GROUP + p, 0)
                centre_row = jnp.where(cross, offsets[section, 0, 0, slot], 0)
                centre_col = jnp.where(cross, offsets[section, 0, 1, slot], 0)
                items.append((pair, source, SLOTS + pair, centre_row, centre_col))
            displace(items)

        return carry

    lax.fori_loop(0, 7, stage, 0)
    finish_seams()

    def drain(copies):
        for copy in copies:
            copy.wait_send()

    @pl.when(has_above)
    def _():
        drain(below_rem + below_main[0] + below_main[1])

    @pl.when(has_left)
    def _():
        drain([left_rem] + left_main)

    @pl.when(has_before)
    def _():
        drain(next_main + next_rem)

    for copy, (there, _, _) in zip(mesh_copies, mesh_peers):

        @pl.when(there)
        def _(copy=copy):
            copy.wait_send()


def local(patches, margins, offsets, counts):
    sections = patches.shape[0]
    hbm = pl.BlockSpec(memory_space=pltpu.HBM)
    vmem = pl.BlockSpec(memory_space=pltpu.VMEM)
    bf16, f32 = jnp.bfloat16, jnp.float32
    flow, seams = (
        pl.pallas_call(
            functools.partial(kernel, sections),
            out_shape=(
                jax.ShapeDtypeStruct((sections, 1, 2, SLOTS), f32),
                jax.ShapeDtypeStruct((sections, 1, 2, EDGES), f32),
            ),
            in_specs=[hbm] * 5,
            out_specs=(vmem, vmem),
            scratch_shapes=[
                pltpu.SMEM((sections, 1, 2, SLOTS), jnp.int32),
                pltpu.SMEM((1, sections), jnp.int32),
                pltpu.VMEM((TABLE_ROWS, 256), bf16),
                pltpu.VMEM((IMAGES, SIDE, LANES), bf16),
                pltpu.VMEM((12, SIDE, LANES), bf16),
                pltpu.VMEM((28, SIDE, TAIL), bf16),
                pltpu.VMEM((IMAGES, 2, BAND, 256), bf16),
                pltpu.VMEM((PAIR_ROWS, 256), f32),
                pltpu.VMEM((PAIR_ROWS, 256), f32),
                pltpu.VMEM((PAIR_ROWS, 256), f32),
                pltpu.VMEM((PAIR_ROWS, 256), jnp.int32),
                pltpu.VMEM((16, LANES), f32),
                pltpu.VMEM((4, 16, LANES), f32),
                pltpu.SemaphoreType.DMA((9,)),
                pltpu.SemaphoreType.DMA((19,)),
                pltpu.SemaphoreType.DMA((19,)),
                pltpu.SemaphoreType.DMA((4,)),
                pltpu.SemaphoreType.DMA((4,)),
                pltpu.SemaphoreType.REGULAR((2,)),
            ],
            compiler_params=pltpu.CompilerParams(
                collective_id=0, has_side_effects=True, vmem_limit_bytes=60 * 1024 * 1024
            ),
        )(patches, margins, jnp.asarray(tables()), jnp.swapaxes(offsets, 2, 3), jnp.swapaxes(counts, 0, 1))
    )
    return tuple(
        pl.pallas_call(
            hand_over,
            out_shape=(
                jax.ShapeDtypeStruct(flow.shape, f32),
                jax.ShapeDtypeStruct(seams.shape, f32),
            ),
            in_specs=[vmem, vmem],
            out_specs=(vmem, vmem),
        )(flow, seams)
    )


def hand_over(flow_in, seams_in, flow_out, seams_out):
    flow_out[...] = flow_in[...]
    seams_out[...] = seams_in[...]


def solution(mesh):
    return jax.shard_map(
        local,
        mesh=mesh,
        in_specs=(
            P("sec", "xy", None, None, None),
            P("sec", "xy", None, None, None),
            P("sec", "xy", None, None),
            P("sec", "xy"),
        ),
        out_specs=(P("sec", "xy", None, None), P("sec", "xy", None, None)),
        check_vma=False,
    )
```

```python
import functools

import jax
import jax.numpy as jnp
import ml_dtypes
import numpy as np
from jax import lax
from jax.experimental import pallas as pl
from jax.experimental.pallas import tpu as pltpu
from jax.sharding import PartitionSpec as P

SIDE = 160
HALF = SIDE // 2
PATCH_ROWS = 2
PATCH_COLS = 4
GRID_COLS = 4
SLOTS = PATCH_ROWS * PATCH_COLS
EDGES = PATCH_ROWS + PATCH_COLS
LANES = 128
TAIL = SIDE - LANES
GROUP = 4
BAND = 96
PIXEL_UNIT = 16.0
LOG2E = 1.4426950408889634
SCORE_SCALE = 2.0 / float(SIDE) ** 3
EXP2_SCALE = SCORE_SCALE * LOG2E

T_ROW = 0
WRE_ROW = T_ROW + 256
WIM_ROW = WRE_ROW + 256
CS_ROW = WIM_ROW + 256
BACK_ROW = CS_ROW + 2 * BAND
TABLE_ROWS = BACK_ROW + SIDE

NEXT = 16
LEFT = 24
BELOW = 28
IMAGES = 36
PAIRS = 28
PAIR_ROWS = 32

MESH = pl.DeviceIdType.MESH


def tables():
    freq = np.arange(SIDE)
    phase = (freq[:, None] * freq[None, :]) % SIDE
    angle = phase.astype(np.float32) * np.float32(2.0 * np.pi / SIDE)
    cosine = np.cos(angle).astype(ml_dtypes.bfloat16).astype(np.float32)
    sine = np.sin(angle).astype(ml_dtypes.bfloat16).astype(np.float32)
    n = HALF + 1
    out = np.zeros((TABLE_ROWS, 256), np.float32)
    right = np.zeros((SIDE, 256), np.float32)
    right[:, :n] = cosine[:, :n]
    right[:, 128 : 128 + n] = sine[:, :n]
    out[T_ROW : T_ROW + SIDE] = right
    inner = np.ones((n, 1), np.float32)
    inner[0] = inner[HALF] = 0.0
    cos_half, sin_half = cosine[:n, :n], sine[:n, :n]
    out[WRE_ROW : WRE_ROW + n, :n] = cos_half
    out[WRE_ROW + 128 : WRE_ROW + 128 + n, :n] = cos_half * inner
    out[WRE_ROW : WRE_ROW + n, 128 : 128 + n] = sin_half
    out[WRE_ROW + 128 : WRE_ROW + 128 + n, 128 : 128 + n] = -sin_half * inner
    out[WIM_ROW : WIM_ROW + n, :n] = sin_half
    out[WIM_ROW + 128 : WIM_ROW + 128 + n, :n] = sin_half * inner
    out[WIM_ROW : WIM_ROW + n, 128 : 128 + n] = cos_half
    out[WIM_ROW + 128 : WIM_ROW + 128 + n, 128 : 128 + n] = -cos_half * inner
    out[CS_ROW : CS_ROW + n, :SIDE] = cosine[:n]
    out[CS_ROW + BAND : CS_ROW + BAND + n, :SIDE] = sine[:n]
    twice = 1.0 + inner[:, 0]
    out[BACK_ROW : BACK_ROW + SIDE, :n] = cosine[:, :n] * twice
    out[BACK_ROW : BACK_ROW + SIDE, BAND : BAND + n] = -sine[:, :n] * twice
    return out.astype(ml_dtypes.bfloat16)


def iota(shape, axis):
    return lax.broadcasted_iota(jnp.int32, shape, axis)


def dot(a, b):
    return jnp.dot(a, b, preferred_element_type=jnp.float32)


def wrapped(index, centre):
    return jnp.where(index >= centre + HALF, index - SIDE, index).astype(jnp.float32)


def kernel(
    sections,
    patches,
    margins,
    table_in,
    offsets_in,
    counts_in,
    flow_out,
    seams_out,
    offsets,
    counts,
    table,
    main,
    rem,
    raw,
    spec,
    peak,
    total,
    moment,
    centre,
    mesh_own,
    mesh_in,
    local_sem,
    send_sem,
    recv_sem,
    mesh_send,
    mesh_recv,
    ready,
):
    sec = lax.axis_index("sec")
    tile = lax.axis_index("xy")
    sec_total = lax.axis_size("sec")
    tile_total = lax.axis_size("xy")
    column = lax.rem(tile, GRID_COLS)
    has_before = sec > 0
    has_after = sec < sec_total - 1
    has_left = column > 0
    has_right = column < GRID_COLS - 1
    has_above = tile >= GRID_COLS
    has_below = tile < tile_total - GRID_COLS
    place = lax.rem(tile, 2 * GRID_COLS)
    host = place >= GRID_COLS
    guest = jnp.logical_not(host)
    turns = (
        jnp.where(place == 0, 1, jnp.where(place == 1, 1, jnp.where(place == 2, 5, jnp.where(place == 3, 1, jnp.where(place == 4, -1, jnp.where(place == 5, -1, jnp.where(place == 6, 2, -1))))))),
        jnp.where(place == 0, 2, jnp.where(place == 1, 1, jnp.where(place == 2, 5, jnp.where(place == 3, 1, jnp.where(place == 4, -1, jnp.where(place == 5, -1, jnp.where(place == 6, 3, -1))))))),
    )

    barrier = pltpu.get_barrier_semaphore()
    beside = (
        (has_before, (sec - 1, tile)),
        (has_after, (sec + 1, tile)),
        (has_left, (sec, tile - 1)),
        (has_right, (sec, tile + 1)),
    )
    across = (
        (has_above, (sec, tile - GRID_COLS), 1),
        (has_below, (sec, tile + GRID_COLS), 0),
    )
    for there, device in beside:

        @pl.when(there)
        def _(device=device):
            pl.semaphore_signal(barrier, inc=1, device_id=device, device_id_type=MESH)

    for there, device, _ in across:

        @pl.when(there & guest)
        def _(device=device):
            pl.semaphore_signal(barrier, inc=1, device_id=device, device_id_type=MESH)

    def transfer(number, src, dst, device):
        return pltpu.make_async_remote_copy(
            src_ref=src,
            dst_ref=dst,
            send_sem=send_sem.at[number],
            recv_sem=recv_sem.at[number],
            device_id=device,
            device_id_type=MESH,
        )

    before, left, above = (sec - 1, tile), (sec, tile - 1), (sec, tile - GRID_COLS)
    below_main = [
        [
            transfer(
                4 * k + c,
                margins.at[k, 0, PATCH_ROWS + c, :, pl.ds(0, LANES)],
                main.at[BELOW + 4 * k + c],
                above,
            )
            for c in range(PATCH_COLS)
        ]
        for k in range(sections)
    ]
    below_rem = [transfer(8 + k, rem.at[9 + 1 + k], rem.at[7 + k], above) for k in range(sections)]
    left_main = [
        transfer(
            10 + 2 * k + r,
            margins.at[k, 0, r, :, pl.ds(0, LANES)],
            main.at[LEFT + 2 * k + r],
            left,
        )
        for k in range(sections)
        for r in range(PATCH_ROWS)
    ]
    left_rem = transfer(14, rem.at[9], rem.at[6], left)
    next_main = [
        transfer(
            15 + h,
            patches.at[0, 0, pl.ds(4 * h, 4), :, pl.ds(0, LANES)],
            main.at[pl.ds(NEXT + 4 * h, 4)],
            before,
        )
        for h in range(2)
    ]
    next_rem = [transfer(17 + h, rem.at[h], rem.at[4 + h], before) for h in range(2)]

    def start(copies):
        for copy in copies:
            copy.start()

    def pack(slot, sources):
        rem[slot] = jnp.concatenate([raw[i] for i in sources], axis=1)

    greeted = functools.reduce(jnp.add, [there.astype(jnp.int32) for there, _ in beside])
    greeted += functools.reduce(jnp.add, [(there & host).astype(jnp.int32) for there, _, _ in across])
    pl.semaphore_wait(barrier, greeted)
    for there, device, side in across:

        @pl.when(there & host)
        def _(device=device, side=side):
            pl.semaphore_signal(ready.at[side], inc=1, device_id=device, device_id_type=MESH)

    @pl.when(has_above & (turns[0] < 0))
    def _():
        start(below_main[0])

    @pl.when(has_left & guest)
    def _():
        start(left_main)

    @pl.when(has_before)
    def _():
        start(next_main)

    local_copies = []

    def fetch(src, dst):
        copy = pltpu.make_async_copy(src, dst, local_sem.at[len(local_copies)])
        copy.start()
        local_copies.append(copy)
        return copy

    margin_raw = [
        fetch(margins.at[k, 0, :, :, pl.ds(LANES, TAIL)], raw.at[pl.ds(16 + EDGES * k, EDGES)])
        for k in range(sections)
    ]
    patch_raw = [
        fetch(patches.at[k, 0, :, :, pl.ds(LANES, TAIL)], raw.at[pl.ds(SLOTS * k, SLOTS)])
        for k in range(sections)
    ]
    patch_main = [
        fetch(patches.at[k, 0, :, :, pl.ds(0, LANES)], main.at[pl.ds(SLOTS * k, SLOTS)])
        for k in range(sections)
    ]
    rest = [fetch(table_in, table), fetch(offsets_in, offsets), fetch(counts_in, counts)]

    for copy in margin_raw:
        copy.wait()
    pack(10, [16 + PATCH_ROWS + c for c in range(4)])
    pack(11, [16 + EDGES + PATCH_ROWS + c for c in range(4)])

    @pl.when(has_above & (turns[0] < 0))
    def _():
        start([below_rem[0]])

    @pl.when(has_above & (turns[1] < 0))
    def _():
        start([below_rem[1]] + below_main[1])

    pack(9, [16, 17, 16 + EDGES, 16 + EDGES + 1])

    @pl.when(has_left & guest)
    def _():
        start([left_rem])

    for copy in patch_raw:
        copy.wait()
    for h in range(4):
        pack(h, [4 * h + p for p in range(4)])

    @pl.when(has_before)
    def _():
        start(next_rem)

    for copy in patch_main + rest:
        copy.wait()

    lane = iota((1, LANES), 1)
    group_of_lane = lane // TAIL

    def spectra(group):
        tail = rem[group].astype(jnp.float32)
        tail_sum = jnp.sum(tail, axis=0, keepdims=True)
        means = []
        for p in range(GROUP):
            sums = jnp.sum(main[GROUP * group + p].astype(jnp.float32), axis=0, keepdims=True)
            sums = sums + jnp.where(group_of_lane == p, tail_sum, 0.0)
            means.append(jnp.sum(sums, axis=1, keepdims=True) * (1.0 / (SIDE * SIDE)))

        def by_lane(values):
            out = jnp.broadcast_to(values[0], (1, LANES))
            for p in range(1, GROUP):
                out = jnp.where(group_of_lane == p, values[p], out)
            return out

        tail = tail - by_lane(means)
        tail_sum = jnp.sum(tail * tail, axis=0, keepdims=True)
        scales = []
        for p in range(GROUP):
            centred = main[GROUP * group + p].astype(jnp.float32) - means[p]
            sums = jnp.sum(centred * centred, axis=0, keepdims=True)
            sums = sums + jnp.where(group_of_lane == p, tail_sum, 0.0)
            variance = jnp.sum(sums, axis=1, keepdims=True) * (1.0 / (SIDE * SIDE))
            scales.append(1.0 / jnp.sqrt(variance + 1e-05))
        tail = tail * by_lane(scales)
        normal = []
        for p in range(GROUP):
            head = (main[GROUP * group + p].astype(jnp.float32) - means[p]) * scales[p]
            rolled = tail if p == 0 else pltpu.roll(tail, LANES - TAIL * p, 1)
            normal.append(jnp.concatenate([head, rolled], axis=1).astype(jnp.bfloat16))
        normal = jnp.concatenate(normal, axis=0)
        rows = dot(normal, table[T_ROW : T_ROW + 256]).astype(jnp.bfloat16)
        for p in range(GROUP):
            image = GROUP * group + p
            both = dot(table[CS_ROW : CS_ROW + 2 * BAND, :SIDE], rows[SIDE * p : SIDE * (p + 1)])
            cc, cs = both[:BAND, :LANES], both[:BAND, LANES:]
            sc, ss = both[BAND:, :LANES], both[BAND:, LANES:]
            spec[image, 0] = jnp.concatenate([cc - ss, cc + ss], axis=1).astype(jnp.bfloat16)
            spec[image, 1] = jnp.concatenate([-(sc + cs), sc - cs], axis=1).astype(jnp.bfloat16)

    shift_rows = iota((SIDE, LANES), 0)

    def displace(items):
        cross_re, cross_im = [], []
        for _, source, target, _, _ in items:
            a_re, a_im = spec[source, 0].astype(jnp.float32), spec[source, 1].astype(jnp.float32)
            b_re, b_im = spec[target, 0].astype(jnp.float32), spec[target, 1].astype(jnp.float32)
            cross_re.append((a_re * b_re + a_im * b_im).astype(jnp.bfloat16))
            cross_im.append((a_im * b_re - a_re * b_im).astype(jnp.bfloat16))
        all_re = dot(jnp.concatenate(cross_re, axis=0), table[WRE_ROW : WRE_ROW + 256])
        all_im = dot(jnp.concatenate(cross_im, axis=0), table[WIM_ROW : WIM_ROW + 256])
        for p, (pair, _, _, centre_row, centre_col) in enumerate(items):
            from_re, from_im = all_re[BAND * p : BAND * (p + 1)], all_im[BAND * p : BAND * (p + 1)]
            u_re, v_re = from_re[:, :LANES], from_re[:, LANES:]
            u_im, v_im = from_im[:, :LANES], from_im[:, LANES:]
            back_u = jnp.concatenate([u_re - u_im, u_re + u_im], axis=1).astype(jnp.bfloat16)
            back_v = jnp.concatenate([v_im + v_re, v_im - v_re], axis=1).astype(jnp.bfloat16)
            scores = dot(
                table[BACK_ROW : BACK_ROW + SIDE, : 2 * BAND],
                jnp.concatenate([back_u, back_v], axis=0),
            )
            largest = jnp.max(scores, axis=0, keepdims=True)
            weights = jnp.exp2((scores - largest) * EXP2_SCALE)
            labels = wrapped(shift_rows, centre_row)
            labels = jnp.concatenate([labels, labels], axis=1)
            peak[pl.ds(pair, 1), :] = largest
            total[pl.ds(pair, 1), :] = jnp.sum(weights, axis=0, keepdims=True)
            moment[pl.ds(pair, 1), :] = jnp.sum(weights * labels, axis=0, keepdims=True)
            centre[pl.ds(pair, 1), :] = jnp.broadcast_to(centre_col, (1, 256))

    def displacements(first, count):
        wide = iota((count, 256), 1)
        near = wide < LANES
        shift = jnp.where(near, wide, SIDE + LANES - wide)
        valid = (near & (wide <= HALF)) | ((wide > LANES) & (wide < LANES + HALF))
        height = jnp.where(valid, peak[first : first + count], -jnp.inf)
        top = jnp.max(height, axis=1, keepdims=True)
        share = jnp.exp2((height - top) * EXP2_SCALE)
        share = jnp.where(valid, share, 0.0)
        mass = share * total[first : first + count]
        whole = jnp.sum(mass, axis=1, keepdims=True)
        labels = wrapped(shift, centre[first : first + count])
        scale = 1.0 / (whole * PIXEL_UNIT)
        rows = jnp.sum(share * moment[first : first + count], axis=1, keepdims=True) * scale
        cols = jnp.sum(mass * labels, axis=1, keepdims=True) * scale
        return rows, cols

    mesh_lane = iota((16, LANES), 1)
    mesh_row = iota((16, LANES), 0)
    mesh_peers = (
        (has_right, has_left, (sec, tile + 1)),
        (has_left, has_right, (sec, tile - 1)),
        (has_below, has_above, (sec, tile + GRID_COLS)),
        (has_above, has_below, (sec, tile - GRID_COLS)),
    )
    mesh_copies = [
        pltpu.make_async_remote_copy(
            src_ref=mesh_own,
            dst_ref=mesh_in.at[i],
            send_sem=mesh_send.at[i],
            recv_sem=mesh_recv.at[i],
            device_id=device,
            device_id_type=MESH,
        )
        for i, (_, _, device) in enumerate(mesh_peers)
    ]

    def send_mesh():
        rows, cols = displacements(0, 16)
        held = jnp.where(mesh_row < SLOTS, counts[0, 0], counts[0, sections - 1])
        last = jnp.where(has_after, 2 * SLOTS, SLOTS)
        usable = ((mesh_row & (SLOTS - 1)) < held) & (mesh_row < last)
        values = jnp.where(mesh_lane == 0, rows, jnp.where(mesh_lane == 1, cols, 1.0))
        mesh_own[...] = jnp.where(usable & (mesh_lane < 3), values, 0.0)
        for copy, (there, _, _) in zip(mesh_copies, mesh_peers):

            @pl.when(there)
            def _(copy=copy):
                copy.start()

    def smooth():
        for i, (copy, (_, comes, _)) in enumerate(zip(mesh_copies, mesh_peers)):

            @pl.when(comes)
            def _(copy=copy):
                copy.wait_recv()

            @pl.when(jnp.logical_not(comes))
            def _(i=i):
                mesh_in[i] = jnp.zeros((16, LANES), jnp.float32)

        beside = []
        for k in range(sections):
            for r in range(PATCH_ROWS):
                for c in range(PATCH_COLS):
                    base = SLOTS * k

                    def at(ref, row, col, base=base):
                        q = base + PATCH_COLS * row + col
                        return ref[q : q + 1]

                    own = mesh_own
                    parts = [
                        at(own, r, c - 1) if c > 0 else at(mesh_in.at[0], r, PATCH_COLS - 1),
                        at(own, r, c + 1) if c < PATCH_COLS - 1 else at(mesh_in.at[1], r, 0),
                        at(own, r - 1, c) if r > 0 else at(mesh_in.at[2], PATCH_ROWS - 1, c),
                        at(own, r + 1, c) if r < PATCH_ROWS - 1 else at(mesh_in.at[3], 0, c),
                    ]
                    beside.append(functools.reduce(jnp.add, parts))
        beside = jnp.concatenate(beside, axis=0)
        own = mesh_own[...]
        value = own[:, 2:3] * (2.0 * own + beside) / (2.0 + beside[:, 2:3])
        for k in range(sections):
            for axis in range(2):
                diagonal = jnp.where(mesh_row == mesh_lane + SLOTS * k, value[:, axis : axis + 1], 0.0)
                flow_out[k, 0, axis : axis + 1, :] = jnp.sum(diagonal, axis=0, keepdims=True)[:, :SLOTS]

    def finish_seams():
        rows, cols = displacements(16, 16)
        row, where = iota((16, LANES), 0), iota((16, LANES), 1)
        usable = ((row < 4) & has_right) | ((row >= 4) & has_below)
        for k in range(sections):
            pick = jnp.where(where < PATCH_ROWS, 2 * k + where, 4 + 4 * k + where - PATCH_ROWS)
            pick = (row == pick) & usable
            for axis, value in enumerate((rows, cols)):
                seam = jnp.sum(jnp.where(pick, value, 0.0), axis=0, keepdims=True)
                seams_out[k, 0, axis : axis + 1, :] = seam[:, :EDGES]

    def own_spectra(group, carry):
        spectra(group)
        return carry

    lax.fori_loop(0, 2, own_spectra, 0)

    def stage(step, carry):
        late = jnp.where(step == 6, 4, step + 1)
        i = jnp.where(host & (step >= 4), late, step)

        for there, _, side in across:

            @pl.when((step == 1) & there & guest)
            def _(side=side):
                pl.semaphore_wait(ready.at[1 - side], 1)

        for k in range(sections):

            @pl.when(has_above & (step == turns[k]))
            def _(k=k):
                start([below_rem[k]] + below_main[k])

        @pl.when(has_left & host & (step == 5))
        def _():
            start([left_rem] + left_main)

        @pl.when((i == 2) & has_after)
        def _():
            next_rem[0].wait_recv()
            next_main[0].wait_recv()

        @pl.when((i == 3) & has_after)
        def _():
            next_rem[1].wait_recv()
            next_main[1].wait_recv()

        @pl.when(step == 4)
        def _():
            send_mesh()

        @pl.when((i == 4) & has_right)
        def _():
            left_rem.wait_recv()
            for copy in left_main:
                copy.wait_recv()

        @pl.when((i == 5) & has_below)
        def _():
            below_rem[0].wait_recv()
            for copy in below_main[0]:
                copy.wait_recv()

        @pl.when(step == 6)
        def _():
            smooth()

        @pl.when((i == 6) & has_below)
        def _():
            below_rem[1].wait_recv()
            for copy in below_main[1]:
                copy.wait_recv()

        there = (
            (i < 2)
            | ((i < 4) & has_after)
            | ((i == 4) & has_right)
            | ((i > 4) & has_below)
        )

        @pl.when(there)
        def _():
            spectra(i + 2)
            items = []
            for p in range(GROUP):
                pair = GROUP * i + p
                cross = i < 4
                left_source = SLOTS * (p // 2) + PATCH_COLS * (p % 2) + PATCH_COLS - 1
                below_source = SLOTS * (i - 5) + PATCH_COLS + p
                source = jnp.where(cross, pair, jnp.where(i == 4, left_source, below_source))
                section = jnp.where(cross, i // 2, 0)
                slot = jnp.where(cross, lax.rem(i, 2) * GROUP + p, 0)
                centre_row = jnp.where(cross, offsets[section, 0, 0, slot], 0)
                centre_col = jnp.where(cross, offsets[section, 0, 1, slot], 0)
                items.append((pair, source, SLOTS + pair, centre_row, centre_col))
            displace(items)

        return carry

    lax.fori_loop(0, 7, stage, 0)
    finish_seams()

    def drain(copies):
        for copy in copies:
            copy.wait_send()

    @pl.when(has_above)
    def _():
        drain(below_rem + below_main[0] + below_main[1])

    @pl.when(has_left)
    def _():
        drain([left_rem] + left_main)

    @pl.when(has_before)
    def _():
        drain(next_main + next_rem)

    for copy, (there, _, _) in zip(mesh_copies, mesh_peers):

        @pl.when(there)
        def _(copy=copy):
            copy.wait_send()


def local(patches, margins, offsets, counts):
    sections = patches.shape[0]
    hbm = pl.BlockSpec(memory_space=pltpu.HBM)
    vmem = pl.BlockSpec(memory_space=pltpu.VMEM)
    bf16, f32 = jnp.bfloat16, jnp.float32
    flow, seams = (
        pl.pallas_call(
            functools.partial(kernel, sections),
            out_shape=(
                jax.ShapeDtypeStruct((sections, 1, 2, SLOTS), f32),
                jax.ShapeDtypeStruct((sections, 1, 2, EDGES), f32),
            ),
            in_specs=[hbm] * 5,
            out_specs=(vmem, vmem),
            scratch_shapes=[
                pltpu.SMEM((sections, 1, 2, SLOTS), jnp.int32),
                pltpu.SMEM((1, sections), jnp.int32),
                pltpu.VMEM((TABLE_ROWS, 256), bf16),
                pltpu.VMEM((IMAGES, SIDE, LANES), bf16),
                pltpu.VMEM((12, SIDE, LANES), bf16),
                pltpu.VMEM((28, SIDE, TAIL), bf16),
                pltpu.VMEM((IMAGES, 2, BAND, 256), bf16),
                pltpu.VMEM((PAIR_ROWS, 256), f32),
                pltpu.VMEM((PAIR_ROWS, 256), f32),
                pltpu.VMEM((PAIR_ROWS, 256), f32),
                pltpu.VMEM((PAIR_ROWS, 256), jnp.int32),
                pltpu.VMEM((16, LANES), f32),
                pltpu.VMEM((4, 16, LANES), f32),
                pltpu.SemaphoreType.DMA((9,)),
                pltpu.SemaphoreType.DMA((19,)),
                pltpu.SemaphoreType.DMA((19,)),
                pltpu.SemaphoreType.DMA((4,)),
                pltpu.SemaphoreType.DMA((4,)),
                pltpu.SemaphoreType.REGULAR((2,)),
            ],
            compiler_params=pltpu.CompilerParams(
                collective_id=0, has_side_effects=True, vmem_limit_bytes=60 * 1024 * 1024
            ),
        )(patches, margins, jnp.asarray(tables()), jnp.swapaxes(offsets, 2, 3), jnp.swapaxes(counts, 0, 1))
    )
    return tuple(
        pl.pallas_call(
            hand_over,
            out_shape=(
                jax.ShapeDtypeStruct(flow.shape, f32),
                jax.ShapeDtypeStruct(seams.shape, f32),
            ),
            in_specs=[vmem, vmem],
            out_specs=(vmem, vmem),
        )(flow, seams)
    )


def hand_over(flow_in, seams_in, flow_out, seams_out):
    flow_out[...] = flow_in[...]
    seams_out[...] = seams_in[...]


def solution(mesh):
    return jax.shard_map(
        local,
        mesh=mesh,
        in_specs=(
            P("sec", "xy", None, None, None),
            P("sec", "xy", None, None, None),
            P("sec", "xy", None, None),
            P("sec", "xy"),
        ),
        out_specs=(P("sec", "xy", None, None), P("sec", "xy", None, None)),
        check_vma=False,
    )
```
